32 devices in a mesh: lp: 2 (over y), row: 4 (over z), col: 4 (over x, core).
Axes of the slice: x: 2, y: 2, z: 4, core: 2. Of those that a mesh axis runs over, the one named last changes fastest.
Arguments:
- tile_values: bfloat16 [8, 4, 16, 256, 256], P(('lp', 'row'), 'col'), parts along dimension 0, may hold values from -0.125 to 0.125
- tile_spots: int32 [8, 4, 16, 2], P(('lp', 'row'), 'col'), parts along dimension 0, may hold values from 0 to 3, as said below
- tile_counts: int32 [8, 4], P(('lp', 'row'), 'col'), parts along dimension 0, may hold values from 1 to 16, as said below
- objective: float32 [8192], P(('lp', 'col')), parts along dimension 0, may hold values from -21 to 21
- lower_bound: float32 [8192], P(('lp', 'col')), parts along dimension 0, may hold values from -1.5 to -0.2
- bound_span: float32 [8192], P(('lp', 'col')), parts along dimension 0, may hold values from 0.5 to 2.5
- var_kind: int32 [8192], P(('lp', 'col')), parts along dimension 0, may hold values from 0 to 3
- right_side: float32 [256, 4096], P('lp', 'row'), parts along dimension 0, may hold values from -63 to 63
- row_kind: int32 [8192], P(('lp', 'row')), parts along dimension 0, may hold values 0 or 1
- primal_start: float32 [256, 4096], P('lp', 'col'), parts along dimension 0, may hold values from -4 to 4
- dual_start: float32 [256, 4096], P('lp', 'row'), parts along dimension 0, may hold values from -4 to 4
Outputs:
- primal_iterate: float32 [256, 4096], P('lp', 'col'), parts along dimension 0
- dual_iterate: float32 [256, 4096], P('lp', 'row'), parts along dimension 0
The draws below stay inside these ranges and needn't reach their ends.
There are 2 independent parts, one for each index of `lp`. The reference program is written for one: setup_inputs(seed, part) draws one part's arguments, and reference() takes and returns one part's arrays. A program takes and returns all parts, laid end to end along the dimension named above; each array names one. Nothing has to cross between parts.
Inputs may be any that keep to these rules, and one draw needn't show every extreme that they name: Slot t of grid cell (r, c) names row block tile_spots[r, c, t, 0] below 4 and column block tile_spots[r, c, t, 1] below 4 of that cell; the slots of one cell name distinct pairs. Slots 0 to tile_counts - 1 of a grid cell hold its tiles; some cell uses all 16 slots.
All inputs are finite; a program needn't handle non-finite values. No bound on the sum of `row_kind` on one device may be relied on, other than what follows from the above.
Results may differ from the reference program's by a relative error of at most 0.0014.
Values sent between devices are 32-bit elements; how exact they have to be, the bound alone decides.
A program may use at most 64 MiB of HBM per device.

```python
import jax
import jax.numpy as jnp
from jax import lax

TILE = 256
RB_DEV = 4
CB_DEV = 4
TILES_DEV = 16
SCEN = 128
ITERS = 3
ROWS = 4096
COLS = 4096
N_ROW = 4
N_COL = 4


def draw_tile_spots(key, part):
    key = jax.random.fold_in(key, 1)
    grid_rows = ROWS // (RB_DEV * TILE)
    grid_cols = COLS // (CB_DEV * TILE)
    cell_keys = jax.random.split(key, grid_rows * grid_cols)
    orders = jax.vmap(lambda one_key: jax.random.permutation(one_key, RB_DEV * CB_DEV))(cell_keys)[:, :TILES_DEV]
    spots = jnp.stack([orders // CB_DEV, orders % CB_DEV], axis=-1)
    return spots.reshape(grid_rows, grid_cols, TILES_DEV, 2).astype(jnp.int32)


def draw_tile_counts(key, part):
    key = jax.random.fold_in(key, 2)
    grid_rows = ROWS // (RB_DEV * TILE)
    grid_cols = COLS // (CB_DEV * TILE)
    first_key, second_key = jax.random.split(key)
    level = jax.random.randint(first_key, (grid_rows * grid_cols,), 0, TILES_DEV)
    counts = 1 + level * level // max(TILES_DEV - 1, 1)
    busiest = jax.random.randint(second_key, (), 0, grid_rows * grid_cols)
    counts = counts.at[busiest].set(TILES_DEV)
    return counts.reshape(grid_rows, grid_cols).astype(jnp.int32)


def draw_objective(key, part):
    key = jax.random.fold_in(key, 3)
    noise_key, factor_key = jax.random.split(key)
    position = jnp.arange(COLS).astype(jnp.float32) / max(COLS - 1, 1)
    profile = 1.0 + 2.0 * position
    factor = jnp.exp(jax.random.uniform(factor_key, (COLS,), minval=jnp.log(0.2), maxval=jnp.log(2.0)))
    noise = jnp.clip(jax.random.normal(noise_key, (COLS,)), -3.5, 3.5)
    return (noise * profile * factor).astype(jnp.float32)


def draw_right_side(key, part):
    key = jax.random.fold_in(key, 4)
    noise_key, factor_key, scale_key = jax.random.split(key, 3)
    position = jnp.arange(ROWS).astype(jnp.float32) / max(ROWS - 1, 1)
    profile = (1.0 + 2.0 * position)[None, :]
    factor = jnp.exp(jax.random.uniform(factor_key, (SCEN, ROWS), minval=jnp.log(0.2), maxval=jnp.log(2.0)))
    scenario_scale = jnp.exp(jax.random.uniform(scale_key, (SCEN, 1), minval=jnp.log(0.3), maxval=jnp.log(3.0)))
    noise = jnp.clip(jax.random.normal(noise_key, (SCEN, ROWS)), -3.5, 3.5)
    return (noise * profile * factor * scenario_scale).astype(jnp.float32)


def set_ends(array, stream_key, smallest, largest):
    extent = array.shape
    index_at = [jax.random.randint(jax.random.fold_in(stream_key, axis), (), 0, extent[axis]) for axis in range(len(extent))]
    array = array.at[tuple(index_at)].set(smallest)
    longest = extent.index(max(extent))
    index_at[longest] = (index_at[longest] + 1) % extent[longest]
    return array.at[tuple(index_at)].set(largest)


def shard_levels(own_key, dims, cuts, smallest, high):
    factor_of, own = 1.0, jax.random.fold_in(own_key, 6)
    for axis_at, parts in cuts:
        heights = jnp.exp(jax.random.uniform(jax.random.fold_in(own, axis_at), (parts,), jnp.float32, smallest / len(cuts), high / len(cuts)))
        factor_of = factor_of * jnp.repeat(heights, dims[axis_at] // parts).reshape([-1 if axis == axis_at else 1 for axis in range(len(dims))])
    return factor_of


def bell_draw(own_key, dims, width, most, shards=(), held_as=jnp.bfloat16):
    result = jax.random.normal(own_key, dims, jnp.float32) * width
    if len(shards) > 0:
        result = shard_levels(own_key, dims, shards, -0.22, 0.18) * result
    return jnp.clip(result, min=-most, max=most).astype(held_as)


def setup_inputs(seed: int = 0, part: int = 0) -> dict:
    key_of = jax.random.split(jax.random.key(seed), 12)
    part_splits = jax.random.split(jax.random.fold_in(key_of[11], part), 12)
    return {
        "tile_values": bell_draw(part_splits[0], (N_ROW, N_COL, TILES_DEV, TILE, TILE), (TILE * CB_DEV * N_COL // 2) ** -0.5, 0.125, ((0, 4), (1, 4))),
        "tile_spots": draw_tile_spots(jax.random.fold_in(jax.random.fold_in(key_of[11], part), 71), part),
        "tile_counts": draw_tile_counts(jax.random.fold_in(jax.random.fold_in(key_of[11], part), 71), part),
        "objective": draw_objective(jax.random.fold_in(jax.random.fold_in(key_of[11], part), 71), part),
        "lower_bound": jnp.clip(-1.5 + 1.3 * jax.random.uniform(part_splits[4], (COLS,), jnp.float32) ** shard_levels(part_splits[4], (COLS,), ((0, 4),), -0.2, 0.2), -1.5, -0.2),
        "bound_span": jnp.clip(0.5 + 2.0 * jax.random.uniform(part_splits[5], (COLS,), jnp.float32) ** shard_levels(part_splits[5], (COLS,), ((0, 4),), -0.2, 0.2), 0.5, 2.5),
        "var_kind": set_ends(jax.random.randint(part_splits[6], (COLS,), 0, 4), jax.random.fold_in(part_splits[6], 1), 0, 3).astype(jnp.int32),
        "right_side": draw_right_side(jax.random.fold_in(jax.random.fold_in(key_of[11], part), 71), part),
        "row_kind": set_ends((jax.random.randint(part_splits[8], (ROWS,), 0, 2) < 1).astype(jnp.int32), jax.random.fold_in(part_splits[8], 1), 0, 1),
        "primal_start": bell_draw(part_splits[9], (SCEN, COLS), 1.0, 4.0, ((1, 4),), jnp.float32),
        "dual_start": bell_draw(part_splits[10], (SCEN, ROWS), 1.0, 4.0, ((1, 4),), jnp.float32),
    }


STEP_SCALE = 0.4
EPSILON = 1e-06

def project_primal(values, lower_bound, upper_bound, var_kind):
    low_on = (var_kind == 1) | (var_kind == 3)
    high_on = (var_kind == 2) | (var_kind == 3)
    values = jnp.where(low_on, jnp.maximum(values, lower_bound), values)
    return jnp.where(high_on, jnp.minimum(values, upper_bound), values)

def project_dual(values, row_kind):
    return jnp.where(row_kind == 1, jnp.maximum(values, 0.0), values)

def pick_matrix(indices, in_use, blocks):
    live_slots = jnp.arange(indices.shape[0]) < in_use
    hits = (indices[:, None] == jnp.arange(blocks)[None, :]) & live_slots[:, None]
    return hits.astype(jnp.float32)

def device_primal(tile_set, places, in_use, extra_block):
    blocks = extra_block.reshape(SCEN, CB_DEV, TILE)
    picked = jnp.take(blocks, places[:, 1], axis=1)
    products = jnp.einsum('tij,ktj->kti', tile_set.astype(jnp.float32), picked, precision=lax.Precision.HIGHEST)
    target = pick_matrix(places[:, 0], in_use, RB_DEV)
    summed = jnp.einsum('tr,kti->kri', target, products, precision=lax.Precision.HIGHEST)
    return summed.reshape(SCEN, RB_DEV * TILE)

def device_dual(tile_set, places, in_use, dual_block):
    blocks = dual_block.reshape(SCEN, RB_DEV, TILE)
    picked = jnp.take(blocks, places[:, 0], axis=1)
    products = jnp.einsum('tij,kti->ktj', tile_set.astype(jnp.float32), picked, precision=lax.Precision.HIGHEST)
    target = pick_matrix(places[:, 1], in_use, CB_DEV)
    summed = jnp.einsum('tc,ktj->kcj', target, products, precision=lax.Precision.HIGHEST)
    return summed.reshape(SCEN, CB_DEV * TILE)

def primal_map(tile_values, tile_spots, tile_counts, extrapolated):
    column_parts = jnp.moveaxis(extrapolated.reshape(SCEN, N_COL, CB_DEV * TILE), 1, 0)

    def one_group(pieces):
        tile_row, spot_row, count_row = pieces
        terms = jax.vmap(device_primal)(tile_row, spot_row, count_row, column_parts)
        return lax.optimization_barrier(jnp.sum(terms, axis=0))
    groups = lax.map(one_group, (tile_values, tile_spots, tile_counts))
    return jnp.moveaxis(groups, 0, 1).reshape(SCEN, ROWS)

def dual_map(tile_values, tile_spots, tile_counts, dual_half):
    row_parts = jnp.moveaxis(dual_half.reshape(SCEN, N_ROW, RB_DEV * TILE), 1, 0)

    def one_group(pieces):
        tile_col, spot_col, count_col = pieces
        terms = jax.vmap(device_dual)(tile_col, spot_col, count_col, row_parts)
        return lax.optimization_barrier(jnp.sum(terms, axis=0))
    groups = lax.map(one_group, (jnp.moveaxis(tile_values, 1, 0), jnp.moveaxis(tile_spots, 1, 0), jnp.moveaxis(tile_counts, 1, 0)))
    return jnp.moveaxis(groups, 0, 1).reshape(SCEN, COLS)

def reference(tile_values, tile_spots, tile_counts, objective, lower_bound, bound_span, var_kind, right_side, row_kind, primal_start, dual_start):
    upper_bound = lower_bound + bound_span
    objective_scale = jnp.sqrt(jnp.sum(objective * objective) / COLS + EPSILON)
    weight = objective_scale / jnp.sqrt(lax.optimization_barrier(jnp.sum(right_side * right_side, axis=1)) / ROWS + EPSILON)
    primal, dual_vec = (primal_start, dual_start)
    for iteration in range(ITERS):
        dual_half = lax.optimization_barrier(dual_vec.astype(jnp.bfloat16)).astype(jnp.float32)
        gradient = dual_map(tile_values, tile_spots, tile_counts, dual_half)
        primal_step = (STEP_SCALE / weight)[:, None]
        primal_next = project_primal(primal - primal_step * (objective - gradient), lower_bound, upper_bound, var_kind)
        extrapolated = lax.optimization_barrier((2.0 * primal_next - primal).astype(jnp.bfloat16)).astype(jnp.float32)
        image = primal_map(tile_values, tile_spots, tile_counts, extrapolated)
        dual_step = (STEP_SCALE * weight)[:, None]
        dual_next = project_dual(dual_vec + dual_step * (right_side - image), row_kind)
        if iteration < ITERS - 1:
            primal_spread = jnp.sqrt(lax.optimization_barrier(jnp.sum((primal_next - primal_start) ** 2, axis=1)) / COLS + EPSILON)
            dual_spread = jnp.sqrt(lax.optimization_barrier(jnp.sum((dual_next - dual_start) ** 2, axis=1)) / ROWS + EPSILON)
            weight = jnp.sqrt(weight * dual_spread / primal_spread)
        primal, dual_vec = (primal_next, dual_next)
    return (primal, dual_vec)
```

```python
import functools

import jax
import jax.numpy as jnp
from jax import lax
from jax.experimental import pallas as pl
from jax.experimental.pallas import tpu as pltpu
from jax.sharding import PartitionSpec as P

ITERS = 3
STEP_SCALE = 0.4
EPSILON = 1e-06
SUB = 8
LANE = 128
MESH = pl.DeviceIdType.MESH


def project_primal(values, lower_bound, upper_bound, var_kind):
    low_on = (var_kind == 1) | (var_kind == 3)
    high_on = (var_kind == 2) | (var_kind == 3)
    values = jnp.where(low_on, jnp.maximum(values, lower_bound), values)
    return jnp.where(high_on, jnp.minimum(values, upper_bound), values)


def project_dual(values, row_kind):
    return jnp.where(row_kind == 1, jnp.maximum(values, 0.0), values)


def weight_update(weight, primal_squares, dual_squares, total_cols, total_rows):
    primal_spread = jnp.sqrt(primal_squares / total_cols + EPSILON)
    dual_spread = jnp.sqrt(dual_squares / total_rows + EPSILON)
    return jnp.sqrt(weight * dual_spread / primal_spread)


def pick_matrix(indices, in_use, blocks):
    live_slots = jnp.arange(indices.shape[0]) < in_use
    hits = (indices[:, None] == jnp.arange(blocks)[None, :]) & live_slots[:, None]
    return hits.astype(jnp.float32)


def primal_product(tile_set, places, in_use, extrapolated, row_blocks):
    scenarios = extrapolated.shape[0]
    tile_width = tile_set.shape[-1]
    blocks = extrapolated.reshape(scenarios, -1, tile_width)
    picked = jnp.take(blocks, places[:, 1], axis=1)
    products = jnp.einsum("tij,ktj->kti", tile_set, picked, preferred_element_type=jnp.float32)
    target = pick_matrix(places[:, 0], in_use, row_blocks)
    summed = jnp.einsum("tr,kti->kri", target, products, precision=lax.Precision.HIGHEST)
    return summed.reshape(scenarios, row_blocks * tile_width)


def dual_product(tile_set, places, in_use, dual_half, col_blocks):
    scenarios = dual_half.shape[0]
    tile_width = tile_set.shape[-1]
    blocks = dual_half.reshape(scenarios, -1, tile_width)
    picked = jnp.take(blocks, places[:, 0], axis=1)
    products = jnp.einsum("tij,kti->ktj", tile_set, picked, preferred_element_type=jnp.float32)
    target = pick_matrix(places[:, 1], in_use, col_blocks)
    summed = jnp.einsum("tc,ktj->kcj", target, products, precision=lax.Precision.HIGHEST)
    return summed.reshape(scenarios, col_blocks * tile_width)


def plain(
    tile_values,
    tile_spots,
    tile_counts,
    objective,
    lower_bound,
    bound_span,
    var_kind,
    right_side,
    row_kind,
    primal_start,
    dual_start,
):
    tile_set = tile_values.reshape(tile_values.shape[2:])
    places = tile_spots.reshape(tile_spots.shape[2:])
    in_use = tile_counts.reshape(())
    tile_width = tile_set.shape[-1]
    row_blocks = right_side.shape[1] // tile_width
    col_blocks = objective.shape[0] // tile_width
    row_groups = lax.axis_size("row")
    col_groups = lax.axis_size("col")
    total_rows = right_side.shape[1] * row_groups
    total_cols = objective.shape[0] * col_groups
    upper_bound = lower_bound + bound_span
    objective_squares = lax.psum(jnp.sum(objective * objective), "col")
    objective_scale = jnp.sqrt(objective_squares / total_cols + EPSILON)
    side_squares = jnp.sum(right_side * right_side, axis=1)
    side_total = lax.psum(side_squares, "row")
    weight = objective_scale / jnp.sqrt(side_total / total_rows + EPSILON)
    primal, dual_vec = (primal_start, dual_start)
    dual_stat = side_squares
    primal_total = None
    for iteration in range(ITERS):
        final = iteration == ITERS - 1
        dual_half = dual_vec.astype(jnp.bfloat16)
        partial_gradient = dual_product(tile_set, places, in_use, dual_half, col_blocks)
        gradient = lax.psum(partial_gradient, "row")
        primal_step = (STEP_SCALE / weight)[:, None]
        primal_next = project_primal(
            primal - primal_step * (objective - gradient), lower_bound, upper_bound, var_kind
        )
        extrapolated = (2.0 * primal_next - primal).astype(jnp.bfloat16)
        partial_image = primal_product(tile_set, places, in_use, extrapolated, row_blocks)
        primal_squares = jnp.sum((primal_next - primal_start) ** 2, axis=1)
        image = lax.psum(partial_image, "col")
        dual_step = (STEP_SCALE * weight)[:, None]
        dual_next = project_dual(dual_vec + dual_step * (right_side - image), row_kind)
        dual_stat = jnp.sum((dual_next - dual_start) ** 2, axis=1)
        if not final:
            primal_total = lax.psum(primal_squares, "col")
            dual_total = lax.psum(dual_stat, "row")
            weight = weight_update(weight, primal_total, dual_total, total_cols, total_rows)
        primal, dual_vec = (primal_next, dual_next)
    return (primal, dual_vec)


def kernel(
    n_row,
    n_col,
    chunks,
    tiles,
    spots,
    counts,
    objective,
    lower,
    span,
    var_kind,
    right_side,
    row_kind,
    primal_start,
    dual_start,
    primal_out,
    dual_out,
    matrix,
    matrix_t,
    primal_all,
    dual_all,
    row_send,
    col_send,
    row_recv,
    col_recv,
    cost_all,
    cost_total,
    row_rs_out,
    row_rs_in,
    row_ag_out,
    row_ag_in,
    col_rs_out,
    col_rs_in,
    col_ag_out,
    col_ag_in,
    cost_out,
    cost_in,
):
    r = lax.axis_index("row")
    c = lax.axis_index("col")
    slots, width = tiles.shape[0], tiles.shape[1]
    n_vars = objective.shape[1]
    n_rows = row_kind.shape[1]
    total_cols = n_vars * n_col
    total_rows = n_rows * n_row
    row_blocks, col_blocks = n_rows // width, n_vars // width
    steps = ITERS * chunks
    part = primal_all.shape[1] * SUB

    def row_peer(d):
        return lax.rem(r + d, n_row)

    def col_peer(d):
        return lax.rem(c + d, n_col)

    def row_copy(src, dst, d, out_sem, in_sem):
        return pltpu.make_async_remote_copy(
            src_ref=src, dst_ref=dst, send_sem=out_sem, recv_sem=in_sem,
            device_id={"row": row_peer(d)}, device_id_type=MESH,
        )

    def col_copy(src, dst, d, out_sem, in_sem):
        return pltpu.make_async_remote_copy(
            src_ref=src, dst_ref=dst, send_sem=out_sem, recv_sem=in_sem,
            device_id={"col": col_peer(d)}, device_id_type=MESH,
        )

    def row_rs(s, d):
        k = lax.rem(s, chunks)
        return row_copy(row_send.at[s, row_peer(d)], row_recv.at[s, d - 1], d,
                        row_rs_out.at[k, d - 1], row_rs_in.at[k, d - 1])

    def col_rs(s, d):
        k = lax.rem(s, chunks)
        return col_copy(col_send.at[s, col_peer(d)], col_recv.at[s, d - 1], d,
                        col_rs_out.at[k, d - 1], col_rs_in.at[k, d - 1])

    def row_ag(s, d):
        k = lax.rem(s, chunks)
        here = primal_all.at[s + chunks, r]
        return row_copy(here, here, d, row_ag_out.at[k, d - 1], row_ag_in.at[k, d - 1])

    def col_ag(s, d):
        k = lax.rem(s, chunks)
        here = dual_all.at[s + chunks, c]
        return col_copy(here, here, d, col_ag_out.at[k, d - 1], col_ag_in.at[k, d - 1])

    def cost_copy(d):
        return col_copy(cost_all.at[0], cost_all.at[d], d, cost_out.at[d - 1], cost_in.at[d - 1])

    barrier = pltpu.get_barrier_semaphore()
    for d in range(1, n_row):
        pl.semaphore_signal(barrier, inc=1, device_id={"row": row_peer(d)}, device_id_type=MESH)
    for d in range(1, n_col):
        pl.semaphore_signal(barrier, inc=1, device_id={"col": col_peer(d)}, device_id_type=MESH)

    costs = objective[...]
    cost_all[0] = jnp.broadcast_to(jnp.sum(costs * costs, axis=1, keepdims=True), (SUB, LANE))

    for k in range(chunks):
        rows = pl.ds(k * part, part)
        shape = (part // SUB, SUB, n_vars)
        primal_all[k, :, :, :n_vars] = primal_start[rows, :].reshape(shape)
        primal_all[k, :, :, n_vars:] = jnp.ones((part // SUB, SUB, LANE), jnp.float32)
        shape = (part // SUB, SUB, n_rows)
        dual_all[k, :, :, :n_rows] = dual_start[rows, :].reshape(shape)
        dual_all[k, :, :, n_rows:] = jnp.ones((part // SUB, SUB, LANE), jnp.float32)

    keys = []
    for t in range(slots):
        key = spots[t, 0] * col_blocks + spots[t, 1]
        keys.append(jnp.where(t < counts[0, 0], key, -1))
    for p in range(row_blocks * col_blocks):
        slot = jnp.int32(0)
        live = jnp.float32(0.0)
        for t in range(slots):
            hit = keys[t] == p
            slot = jnp.where(hit, jnp.int32(t), slot)
            live = jnp.where(hit, jnp.float32(1.0), live)
        rb, cb = p // col_blocks, p % col_blocks
        tile = (tiles[slot].astype(jnp.float32) * live).astype(jnp.bfloat16)
        matrix[rb * width:(rb + 1) * width, cb * width:(cb + 1) * width] = tile

    pl.semaphore_wait(barrier, n_row + n_col - 2)
    for d in range(1, n_col):
        cost_copy(d).start()

    def wide(value, width_):
        return jnp.concatenate([value] * (width_ // LANE), axis=1)

    def gradient_part(s):
        k = lax.rem(s, chunks)
        held = dual_all[s, :, :, :n_rows].reshape(part, n_rows)
        first = dual_all[k, :, :, :n_rows].reshape(part, n_rows)
        side = right_side[pl.ds(pl.multiple_of(k * part, part), part), :]
        gap = jnp.where(s < chunks, side, held - first)
        squares = jnp.sum(gap * gap, axis=1, keepdims=True)
        terms = jnp.dot(held.astype(jnp.bfloat16), matrix[...], preferred_element_type=jnp.float32)
        row_send[s, :, :, :n_vars] = terms.reshape(part // SUB, SUB, n_vars)
        row_send[s, :, :, n_vars:] = jnp.broadcast_to(squares, (part, LANE)).reshape(part // SUB, SUB, LANE)
        for d in range(1, n_row):
            row_rs(s, d).start()

    def primal_step(s):
        for d in range(1, n_row):
            row_rs(s, d).wait()
        total = row_send[s, r]
        for d in range(1, n_row):
            total = total + row_recv[s, d - 1]
        gradient, dual_total = total[:, :n_vars], total[:, n_vars:]
        held = primal_all[s, r]
        old, old_weight = held[:, :n_vars], held[:, n_vars:]
        primal_total = dual_all[s, r, :, n_rows:]
        dual_spread = jnp.sqrt(dual_total / total_rows + EPSILON)
        scale = jnp.sqrt(cost_total[...] / total_cols + EPSILON)
        primal_spread = jnp.sqrt(primal_total / total_cols + EPSILON)
        later = jnp.sqrt(old_weight * dual_spread / primal_spread)
        weight = jnp.where(s < chunks, scale / dual_spread, later)
        step = wide(STEP_SCALE / weight, n_vars)
        low = lower[...]
        new = old - step * (objective[...] - gradient)
        new = project_primal(new, low, low + span[...], var_kind[...])
        primal_all[s + chunks, r, :, :n_vars] = new
        primal_all[s + chunks, r, :, n_vars:] = weight
        for d in range(1, n_row):
            row_ag(s, d).start()

    def image_part(s):
        k = lax.rem(s, chunks)
        for d in range(1, n_row):
            row_ag(s, d).wait()
        new = primal_all[s + chunks, :, :, :n_vars].reshape(part, n_vars)
        old = primal_all[s, :, :, :n_vars].reshape(part, n_vars)
        gap = new - primal_all[k, :, :, :n_vars].reshape(part, n_vars)
        squares = jnp.sum(gap * gap, axis=1, keepdims=True)
        ahead = (2.0 * new - old).astype(jnp.bfloat16)
        terms = jnp.dot(ahead, matrix_t[...], preferred_element_type=jnp.float32)
        col_send[s, :, :, :n_rows] = terms.reshape(part // SUB, SUB, n_rows)
        col_send[s, :, :, n_rows:] = jnp.broadcast_to(squares, (part, LANE)).reshape(part // SUB, SUB, LANE)
        for d in range(1, n_col):
            col_rs(s, d).start()
        primal_out[pl.ds(pl.multiple_of(k * part, part), part), :] = new

    def dual_step(s):
        for d in range(1, n_col):
            col_rs(s, d).wait()
        total = col_send[s, c]
        for d in range(1, n_col):
            total = total + col_recv[s, d - 1]
        k = lax.rem(s, chunks)
        at = k * part + c * SUB
        side = right_side[pl.ds(pl.multiple_of(at, SUB), SUB), :]
        step = wide(STEP_SCALE * primal_all[s + chunks, c, :, n_vars:], n_rows)
        new = dual_all[s, c, :, :n_rows] + step * (side - total[:, :n_rows])
        new = project_dual(new, row_kind[...])
        dual_all[s + chunks, c, :, :n_rows] = new
        dual_all[s + chunks, c, :, n_rows:] = total[:, n_rows:]
        for d in range(1, n_col):
            col_ag(s, d).start()

    def dual_arrive(s):
        for d in range(1, n_col):
            col_ag(s, d).wait()

        @pl.when(s >= steps - chunks)
        def _():
            k = lax.rem(s, chunks)
            new = dual_all[s + chunks, :, :, :n_rows].reshape(part, n_rows)
            dual_out[pl.ds(pl.multiple_of(k * part, part), part), :] = new

    def one_step(t, carry):
        @pl.when(t >= 4)
        def _():
            dual_arrive(t - 4)

        @pl.when(t < steps)
        def _():
            gradient_part(t)

        @pl.when(t == 0)
        def _():
            for rb in range(row_blocks):
                for cb in range(col_blocks):
                    tile = matrix[rb * width:(rb + 1) * width, cb * width:(cb + 1) * width]
                    matrix_t[cb * width:(cb + 1) * width, rb * width:(rb + 1) * width] = tile.T
            for d in range(1, n_col):
                cost_copy(d).wait()
            total = cost_all[0]
            for d in range(1, n_col):
                total = total + cost_all[d]
            cost_total[...] = total

        @pl.when((t >= 3) & (t < steps + 3))
        def _():
            dual_step(t - 3)

        @pl.when((t >= 2) & (t < steps + 2))
        def _():
            image_part(t - 2)

        @pl.when((t >= 1) & (t < steps + 1))
        def _():
            primal_step(t - 1)

        return carry

    lax.fori_loop(0, steps + 4, one_step, 0)


def fused(
    tile_values,
    tile_spots,
    tile_counts,
    objective,
    lower_bound,
    bound_span,
    var_kind,
    right_side,
    row_kind,
    primal_start,
    dual_start,
):
    n_row, n_col = lax.axis_size("row"), lax.axis_size("col")
    scenarios, n_rows = right_side.shape
    n_vars = objective.shape[0]
    owners = n_row
    chunks = scenarios // (SUB * owners)
    steps = ITERS * chunks
    vmem = pl.BlockSpec(memory_space=pltpu.VMEM)
    smem = pl.BlockSpec(memory_space=pltpu.SMEM)
    floats = lambda *shape: pltpu.VMEM(shape, jnp.float32)
    sems = lambda *shape: pltpu.SemaphoreType.DMA(shape)
    wide_v, wide_r = n_vars + LANE, n_rows + LANE
    return pl.pallas_call(
        functools.partial(kernel, n_row, n_col, chunks),
        out_shape=(
            jax.ShapeDtypeStruct(primal_start.shape, jnp.float32),
            jax.ShapeDtypeStruct(dual_start.shape, jnp.float32),
        ),
        in_specs=[vmem, smem, smem] + [vmem] * 8,
        out_specs=(vmem, vmem),
        scratch_shapes=[
            pltpu.VMEM((n_rows, n_vars), jnp.bfloat16),
            pltpu.VMEM((n_vars, n_rows), jnp.bfloat16),
            floats(steps + chunks, owners, SUB, wide_v),
            floats(steps + chunks, owners, SUB, wide_r),
            floats(steps, owners, SUB, wide_v),
            floats(steps, owners, SUB, wide_r),
            floats(steps, n_row - 1, SUB, wide_v),
            floats(steps, n_col - 1, SUB, wide_r),
            floats(n_col, SUB, LANE),
            floats(SUB, LANE),
            sems(chunks, n_row - 1), sems(chunks, n_row - 1),
            sems(chunks, n_row - 1), sems(chunks, n_row - 1),
            sems(chunks, n_col - 1), sems(chunks, n_col - 1),
            sems(chunks, n_col - 1), sems(chunks, n_col - 1),
            sems(n_col - 1), sems(n_col - 1),
        ],
        compiler_params=pltpu.CompilerParams(
            collective_id=0, has_side_effects=True, vmem_limit_bytes=48 * 2**20
        ),
    )(
        tile_values.reshape(tile_values.shape[2:]),
        tile_spots.reshape(tile_spots.shape[2:]),
        tile_counts,
        objective.reshape(1, -1),
        lower_bound.reshape(1, -1),
        bound_span.reshape(1, -1),
        var_kind.reshape(1, -1),
        right_side,
        row_kind.reshape(1, -1),
        primal_start,
        dual_start,
    )


def local(*args):
    n_row, n_col = lax.axis_size("row"), lax.axis_size("col")
    scenarios = args[7].shape[0]
    if n_row == n_col and scenarios == SUB * n_row * 4:
        return fused(*args)
    return plain(*args)


def solution(mesh):
    placed = (
        P(("lp", "row"), "col", None, None, None),
        P(("lp", "row"), "col", None, None),
        P(("lp", "row"), "col"),
        P(("lp", "col")),
        P(("lp", "col")),
        P(("lp", "col")),
        P(("lp", "col")),
        P("lp", "row"),
        P(("lp", "row")),
        P("lp", "col"),
        P("lp", "row"),
    )
    return jax.shard_map(
        local,
        mesh=mesh,
        in_specs=placed,
        out_specs=(P("lp", "col"), P("lp", "row")),
        check_vma=False,
    )
```

```python
import functools

import jax
import jax.numpy as jnp
from jax import lax
from jax.experimental import pallas as pl
from jax.experimental.pallas import tpu as pltpu
from jax.sharding import PartitionSpec as P

ITERS = 3
STEP_SCALE = 0.4
EPSILON = 1e-06
SUB = 4
LANE = 128
MESH = pl.DeviceIdType.MESH


def project_primal(values, lower_bound, upper_bound, var_kind):
    low_on = (var_kind == 1) | (var_kind == 3)
    high_on = (var_kind == 2) | (var_kind == 3)
    values = jnp.where(low_on, jnp.maximum(values, lower_bound), values)
    return jnp.where(high_on, jnp.minimum(values, upper_bound), values)


def project_dual(values, row_kind):
    return jnp.where(row_kind == 1, jnp.maximum(values, 0.0), values)


def weight_update(weight, primal_squares, dual_squares, total_cols, total_rows):
    primal_spread = jnp.sqrt(primal_squares / total_cols + EPSILON)
    dual_spread = jnp.sqrt(dual_squares / total_rows + EPSILON)
    return jnp.sqrt(weight * dual_spread / primal_spread)


def pick_matrix(indices, in_use, blocks):
    live_slots = jnp.arange(indices.shape[0]) < in_use
    hits = (indices[:, None] == jnp.arange(blocks)[None, :]) & live_slots[:, None]
    return hits.astype(jnp.float32)


def primal_product(tile_set, places, in_use, extrapolated, row_blocks):
    scenarios = extrapolated.shape[0]
    tile_width = tile_set.shape[-1]
    blocks = extrapolated.reshape(scenarios, -1, tile_width)
    picked = jnp.take(blocks, places[:, 1], axis=1)
    products = jnp.einsum("tij,ktj->kti", tile_set, picked, preferred_element_type=jnp.float32)
    target = pick_matrix(places[:, 0], in_use, row_blocks)
    summed = jnp.einsum("tr,kti->kri", target, products, precision=lax.Precision.HIGHEST)
    return summed.reshape(scenarios, row_blocks * tile_width)


def dual_product(tile_set, places, in_use, dual_half, col_blocks):
    scenarios = dual_half.shape[0]
    tile_width = tile_set.shape[-1]
    blocks = dual_half.reshape(scenarios, -1, tile_width)
    picked = jnp.take(blocks, places[:, 0], axis=1)
    products = jnp.einsum("tij,kti->ktj", tile_set, picked, preferred_element_type=jnp.float32)
    target = pick_matrix(places[:, 1], in_use, col_blocks)
    summed = jnp.einsum("tc,ktj->kcj", target, products, precision=lax.Precision.HIGHEST)
    return summed.reshape(scenarios, col_blocks * tile_width)


def plain(
    tile_values,
    tile_spots,
    tile_counts,
    objective,
    lower_bound,
    bound_span,
    var_kind,
    right_side,
    row_kind,
    primal_start,
    dual_start,
):
    tile_set = tile_values.reshape(tile_values.shape[2:])
    places = tile_spots.reshape(tile_spots.shape[2:])
    in_use = tile_counts.reshape(())
    tile_width = tile_set.shape[-1]
    row_blocks = right_side.shape[1] // tile_width
    col_blocks = objective.shape[0] // tile_width
    row_groups = lax.axis_size("row")
    col_groups = lax.axis_size("col")
    total_rows = right_side.shape[1] * row_groups
    total_cols = objective.shape[0] * col_groups
    upper_bound = lower_bound + bound_span
    objective_squares = lax.psum(jnp.sum(objective * objective), "col")
    objective_scale = jnp.sqrt(objective_squares / total_cols + EPSILON)
    side_squares = jnp.sum(right_side * right_side, axis=1)
    side_total = lax.psum(side_squares, "row")
    weight = objective_scale / jnp.sqrt(side_total / total_rows + EPSILON)
    primal, dual_vec = (primal_start, dual_start)
    dual_stat = side_squares
    primal_total = None
    for iteration in range(ITERS):
        final = iteration == ITERS - 1
        dual_half = dual_vec.astype(jnp.bfloat16)
        partial_gradient = dual_product(tile_set, places, in_use, dual_half, col_blocks)
        gradient = lax.psum(partial_gradient, "row")
        primal_step = (STEP_SCALE / weight)[:, None]
        primal_next = project_primal(
            primal - primal_step * (objective - gradient), lower_bound, upper_bound, var_kind
        )
        extrapolated = (2.0 * primal_next - primal).astype(jnp.bfloat16)
        partial_image = primal_product(tile_set, places, in_use, extrapolated, row_blocks)
        primal_squares = jnp.sum((primal_next - primal_start) ** 2, axis=1)
        image = lax.psum(partial_image, "col")
        dual_step = (STEP_SCALE * weight)[:, None]
        dual_next = project_dual(dual_vec + dual_step * (right_side - image), row_kind)
        dual_stat = jnp.sum((dual_next - dual_start) ** 2, axis=1)
        if not final:
            primal_total = lax.psum(primal_squares, "col")
            dual_total = lax.psum(dual_stat, "row")
            weight = weight_update(weight, primal_total, dual_total, total_cols, total_rows)
        primal, dual_vec = (primal_next, dual_next)
    return (primal, dual_vec)


def kernel(
    n_row,
    n_col,
    chunks,
    tiles_hbm,
    spots,
    counts,
    objective_hbm,
    lower_hbm,
    span_hbm,
    var_kind_hbm,
    right_side_hbm,
    row_kind_hbm,
    primal_start_hbm,
    dual_start_hbm,
    primal_out,
    dual_out,
    tiles,
    objective,
    lower,
    span,
    var_kind,
    right_side,
    row_kind,
    primal_start,
    dual_start,
    sides,
    load_sem,
    matrix,
    matrix_t,
    primal_all,
    dual_all,
    row_send,
    col_send,
    row_mid,
    row_pass,
    row_recv,
    col_recv,
    cost_all,
    cost_total,
    row_rs_out,
    row_rs_in,
    row_ag_out,
    row_ag_in,
    col_rs_out,
    col_rs_in,
    col_ag_out,
    col_ag_in,
    cost_out,
    cost_in,
):
    r = lax.axis_index("row")
    c = lax.axis_index("col")
    odd, upper = lax.rem(r, 2), r // 2
    slots, width = tiles.shape[0], tiles.shape[1]
    n_vars = objective.shape[1]
    n_rows = row_kind.shape[1]
    total_cols = n_vars * n_col
    total_rows = n_rows * n_row
    row_blocks, col_blocks = n_rows // width, n_vars // width
    steps = ITERS * chunks
    part = primal_all.shape[1] * SUB

    def row_peer(d):
        return lax.rem(r + d, n_row)

    def col_peer(d):
        return lax.rem(c + d, n_col)

    def row_copy(src, dst, d, out_sem, in_sem):
        return pltpu.make_async_remote_copy(
            src_ref=src, dst_ref=dst, send_sem=out_sem, recv_sem=in_sem,
            device_id={"row": row_peer(d)}, device_id_type=MESH,
        )

    def col_copy(src, dst, d, out_sem, in_sem):
        return pltpu.make_async_remote_copy(
            src_ref=src, dst_ref=dst, send_sem=out_sem, recv_sem=in_sem,
            device_id={"col": col_peer(d)}, device_id_type=MESH,
        )

    def pair_rs(s):
        k = lax.rem(s, chunks)
        return pltpu.make_async_remote_copy(
            src_ref=row_send.at[s, 1 - odd], dst_ref=row_mid.at[s],
            send_sem=row_rs_out.at[k, 0], recv_sem=row_rs_in.at[k, 0],
            device_id={"row": r + 1 - 2 * odd}, device_id_type=MESH,
        )

    def half_rs(s):
        k = lax.rem(s, chunks)
        return row_copy(row_pass.at[s], row_recv.at[s], n_row // 2,
                        row_rs_out.at[k, 1], row_rs_in.at[k, 1])

    def col_rs(s, d):
        k = lax.rem(s, chunks)
        return col_copy(col_send.at[s, col_peer(d)], col_recv.at[s, d - 1], d,
                        col_rs_out.at[k, d - 1], col_rs_in.at[k, d - 1])

    def row_ag(s, d):
        k = lax.rem(s, chunks)
        here = primal_all.at[s + chunks, r]
        return row_copy(here, here, d, row_ag_out.at[k, d - 1], row_ag_in.at[k, d - 1])

    def col_ag(s, d):
        k = lax.rem(s, chunks)
        here = dual_all.at[s + chunks, c]
        return col_copy(here, here, d, col_ag_out.at[k, d - 1], col_ag_in.at[k, d - 1])

    def cost_copy(d):
        return col_copy(cost_all.at[0], cost_all.at[d], d, cost_out.at[d - 1], cost_in.at[d - 1])

    loads = [
        (tiles_hbm, tiles),
        (dual_start_hbm, dual_start),
        (right_side_hbm, right_side),
        (objective_hbm, objective),
        (primal_start_hbm, primal_start),
        (lower_hbm, lower),
        (span_hbm, span),
        (var_kind_hbm, var_kind),
        (row_kind_hbm, row_kind),
    ]
    loads = [pltpu.make_async_copy(src, dst, load_sem.at[i]) for i, (src, dst) in enumerate(loads)]
    for load in loads:
        load.start()

    barrier = pltpu.get_barrier_semaphore()
    for d in range(1, n_row):
        pl.semaphore_signal(barrier, inc=1, device_id={"row": row_peer(d)}, device_id_type=MESH)
    for d in range(1, n_col):
        pl.semaphore_signal(barrier, inc=1, device_id={"col": col_peer(d)}, device_id_type=MESH)

    for k in range(chunks):
        primal_all[k, :, :, n_vars:] = jnp.ones((part // SUB, SUB, LANE), jnp.float32)
        dual_all[k, :, :, n_rows:] = jnp.ones((part // SUB, SUB, LANE), jnp.float32)

    keys = []
    for t in range(slots):
        key = spots[t, 0] * col_blocks + spots[t, 1]
        keys.append(jnp.where(t < counts[0, 0], key, -1))
    loads[0].wait()
    for p in range(row_blocks * col_blocks):
        slot = jnp.int32(0)
        live = jnp.float32(0.0)
        for t in range(slots):
            hit = keys[t] == p
            slot = jnp.where(hit, jnp.int32(t), slot)
            live = jnp.where(hit, jnp.float32(1.0), live)
        rb, cb = p // col_blocks, p % col_blocks
        tile = (tiles[slot].astype(jnp.float32) * live).astype(jnp.bfloat16)
        matrix[rb * width:(rb + 1) * width, cb * width:(cb + 1) * width] = tile

    for load in loads[1:]:
        load.wait()
    costs = objective[...]
    cost_all[0] = jnp.broadcast_to(jnp.sum(costs * costs, axis=1, keepdims=True), (SUB, LANE))

    for k in range(chunks):
        for q in range(n_row):
            rows = slice(k * part + q * SUB, k * part + (q + 1) * SUB)
            primal_all[k, q, :, :n_vars] = primal_start[rows, :]
            dual_all[k, q, :, :n_rows] = dual_start[rows, :]
            sides[k, q] = right_side[rows, :]
    pl.semaphore_wait(barrier, n_row + n_col - 2)
    for d in range(1, n_col):
        cost_copy(d).start()

    def wide(value, width_):
        return jnp.concatenate([value] * (width_ // LANE), axis=1)

    def stacked(value):
        return jnp.concatenate([value[q] for q in range(value.shape[0])], axis=0)

    def gradient_part(s):
        k = lax.rem(s, chunks)
        held = dual_all[s, :, :, :n_rows]
        gap = jnp.where(s < chunks, sides[k], held - dual_all[k, :, :, :n_rows])
        spread = jnp.broadcast_to(jnp.sum(gap * gap, axis=2, keepdims=True), (n_row, SUB, LANE))
        terms = jnp.dot(stacked(held).astype(jnp.bfloat16), matrix[...], preferred_element_type=jnp.float32)
        for q in range(n_row):
            row_send[s, q % 2, q // 2, :, :n_vars] = terms[q * SUB:(q + 1) * SUB]
            row_send[s, q % 2, q // 2, :, n_vars:] = spread[q]
        pair_rs(s).start()

    def pass_on(s):
        pair_rs(s).wait()
        row_pass[s] = row_send[s, odd, 1 - upper] + row_mid[s, 1 - upper]
        half_rs(s).start()

    def primal_step(s):
        half_rs(s).wait()
        total = row_send[s, odd, upper] + row_mid[s, upper] + row_recv[s]
        gradient, dual_total = total[:, :n_vars], total[:, n_vars:]
        held = primal_all[s, r]
        old, old_weight = held[:, :n_vars], held[:, n_vars:]
        primal_total = dual_all[s, r, :, n_rows:]
        dual_spread = jnp.sqrt(dual_total / total_rows + EPSILON)
        scale = jnp.sqrt(cost_total[...] / total_cols + EPSILON)
        primal_spread = jnp.sqrt(primal_total / total_cols + EPSILON)
        later = jnp.sqrt(old_weight * dual_spread / primal_spread)
        weight = jnp.where(s < chunks, scale / dual_spread, later)
        step = wide(STEP_SCALE / weight, n_vars)
        low = lower[...]
        new = old - step * (objective[...] - gradient)
        new = project_primal(new, low, low + span[...], var_kind[...])
        primal_all[s + chunks, r, :, :n_vars] = new
        primal_all[s + chunks, r, :, n_vars:] = weight
        for d in range(1, n_row):
            row_ag(s, d).start()

    def image_part(s):
        k = lax.rem(s, chunks)
        for d in range(1, n_row):
            row_ag(s, d).wait()
        new = primal_all[s + chunks, :, :, :n_vars]
        old = primal_all[s, :, :, :n_vars]
        gap = new - primal_all[k, :, :, :n_vars]
        spread = jnp.broadcast_to(jnp.sum(gap * gap, axis=2, keepdims=True), (n_row, SUB, LANE))
        ahead = stacked(2.0 * new - old).astype(jnp.bfloat16)
        terms = jnp.dot(ahead, matrix_t[...], preferred_element_type=jnp.float32)
        for q in range(n_col):
            col_send[s, q, :, :n_rows] = terms[q * SUB:(q + 1) * SUB]
            col_send[s, q, :, n_rows:] = spread[q]
        for d in range(1, n_col):
            col_rs(s, d).start()

        @pl.when(s >= steps - chunks)
        def _():
            primal_out[pl.ds(pl.multiple_of(k * part, part), part), :] = stacked(new)

    def dual_step(s):
        for d in range(1, n_col):
            col_rs(s, d).wait()
        total = col_send[s, c]
        for d in range(1, n_col):
            total = total + col_recv[s, d - 1]
        k = lax.rem(s, chunks)
        side = sides[k, c]
        step = wide(STEP_SCALE * primal_all[s + chunks, c, :, n_vars:], n_rows)
        new = dual_all[s, c, :, :n_rows] + step * (side - total[:, :n_rows])
        new = project_dual(new, row_kind[...])
        dual_all[s + chunks, c, :, :n_rows] = new
        dual_all[s + chunks, c, :, n_rows:] = total[:, n_rows:]
        for d in range(1, n_col):
            col_ag(s, d).start()

    def dual_arrive(s):
        for d in range(1, n_col):
            col_ag(s, d).wait()

        @pl.when(s >= steps - chunks)
        def _():
            k = lax.rem(s, chunks)
            new = stacked(dual_all[s + chunks, :, :, :n_rows])
            dual_out[pl.ds(pl.multiple_of(k * part, part), part), :] = new

    def one_step(t, carry):
        def stage(delay, run):
            @pl.when((t >= delay) & (t < steps + delay))
            def _():
                run(t - delay)

        stage(chunks, dual_arrive)
        stage(0, gradient_part)

        @pl.when(t == 0)
        def _():
            for rb in range(row_blocks):
                for cb in range(col_blocks):
                    tile = matrix[rb * width:(rb + 1) * width, cb * width:(cb + 1) * width]
                    matrix_t[cb * width:(cb + 1) * width, rb * width:(rb + 1) * width] = tile.T
            for d in range(1, n_col):
                cost_copy(d).wait()
            total = cost_all[0]
            for d in range(1, n_col):
                total = total + cost_all[d]
            cost_total[...] = total

        stage(3, primal_step)
        stage(6, dual_step)
        stage(1, pass_on)
        stage(4, image_part)
        return carry

    lax.fori_loop(0, steps + chunks, one_step, 0)


def fused(
    tile_values,
    tile_spots,
    tile_counts,
    objective,
    lower_bound,
    bound_span,
    var_kind,
    right_side,
    row_kind,
    primal_start,
    dual_start,
):
    n_row, n_col = lax.axis_size("row"), lax.axis_size("col")
    scenarios, n_rows = right_side.shape
    n_vars = objective.shape[0]
    owners = n_row
    chunks = scenarios // (SUB * owners)
    steps = ITERS * chunks
    vmem = pl.BlockSpec(memory_space=pltpu.VMEM)
    smem = pl.BlockSpec(memory_space=pltpu.SMEM)
    hbm = pl.BlockSpec(memory_space=pltpu.HBM)
    floats = lambda *shape: pltpu.VMEM(shape, jnp.float32)
    sems = lambda *shape: pltpu.SemaphoreType.DMA(shape)
    wide_v, wide_r = n_vars + LANE, n_rows + LANE
    return pl.pallas_call(
        functools.partial(kernel, n_row, n_col, chunks),
        out_shape=(
            jax.ShapeDtypeStruct(primal_start.shape, jnp.float32),
            jax.ShapeDtypeStruct(dual_start.shape, jnp.float32),
        ),
        in_specs=[hbm, smem, smem] + [hbm] * 8,
        out_specs=(vmem, vmem),
        scratch_shapes=[
            pltpu.VMEM(tile_values.shape[2:], jnp.bfloat16),
            floats(1, n_vars),
            floats(1, n_vars),
            floats(1, n_vars),
            pltpu.VMEM((1, n_vars), jnp.int32),
            floats(*right_side.shape),
            pltpu.VMEM((1, n_rows), jnp.int32),
            floats(*primal_start.shape),
            floats(*dual_start.shape),
            floats(chunks, owners, SUB, n_rows),
            sems(9),
            pltpu.VMEM((n_rows, n_vars), jnp.bfloat16),
            pltpu.VMEM((n_vars, n_rows), jnp.bfloat16),
            floats(steps + chunks, owners, SUB, wide_v),
            floats(steps + chunks, owners, SUB, wide_r),
            floats(steps, 2, n_row // 2, SUB, wide_v),
            floats(steps, owners, SUB, wide_r),
            floats(steps, n_row // 2, SUB, wide_v),
            floats(steps, SUB, wide_v),
            floats(steps, SUB, wide_v),
            floats(steps, n_col - 1, SUB, wide_r),
            floats(n_col, SUB, LANE),
            floats(SUB, LANE),
            sems(chunks, 2), sems(chunks, 2),
            sems(chunks, n_row - 1), sems(chunks, n_row - 1),
            sems(chunks, n_col - 1), sems(chunks, n_col - 1),
            sems(chunks, n_col - 1), sems(chunks, n_col - 1),
            sems(n_col - 1), sems(n_col - 1),
        ],
        compiler_params=pltpu.CompilerParams(
            collective_id=0, has_side_effects=True, vmem_limit_bytes=60 * 2**20
        ),
    )(
        tile_values.reshape(tile_values.shape[2:]),
        tile_spots.reshape(tile_spots.shape[2:]),
        tile_counts,
        objective.reshape(1, -1),
        lower_bound.reshape(1, -1),
        bound_span.reshape(1, -1),
        var_kind.reshape(1, -1),
        right_side,
        row_kind.reshape(1, -1),
        primal_start,
        dual_start,
    )


def local(*args):
    n_row, n_col = lax.axis_size("row"), lax.axis_size("col")
    scenarios = args[7].shape[0]
    if n_row == n_col and scenarios == SUB * n_row * 8:
        return fused(*args)
    return plain(*args)


def solution(mesh):
    placed = (
        P(("lp", "row"), "col", None, None, None),
        P(("lp", "row"), "col", None, None),
        P(("lp", "row"), "col"),
        P(("lp", "col")),
        P(("lp", "col")),
        P(("lp", "col")),
        P(("lp", "col")),
        P("lp", "row"),
        P(("lp", "row")),
        P("lp", "col"),
        P("lp", "row"),
    )
    return jax.shard_map(
        local,
        mesh=mesh,
        in_specs=placed,
        out_specs=(P("lp", "col"), P("lp", "row")),
        check_vma=False,
    )
```

```python
import functools

import jax
import jax.numpy as jnp
from jax import lax
from jax.experimental import pallas as pl
from jax.experimental.pallas import tpu as pltpu
from jax.sharding import PartitionSpec as P

ITERS = 3
STEP_SCALE = 0.4
EPSILON = 1e-06
SUB = 4
LANE = 128
MESH = pl.DeviceIdType.MESH


def project_primal(values, lower_bound, upper_bound, var_kind):
    low_on = (var_kind == 1) | (var_kind == 3)
    high_on = (var_kind == 2) | (var_kind == 3)
    values = jnp.where(low_on, jnp.maximum(values, lower_bound), values)
    return jnp.where(high_on, jnp.minimum(values, upper_bound), values)


def project_dual(values, row_kind):
    return jnp.where(row_kind == 1, jnp.maximum(values, 0.0), values)


def weight_update(weight, primal_squares, dual_squares, total_cols, total_rows):
    primal_spread = jnp.sqrt(primal_squares / total_cols + EPSILON)
    dual_spread = jnp.sqrt(dual_squares / total_rows + EPSILON)
    return jnp.sqrt(weight * dual_spread / primal_spread)


def pick_matrix(indices, in_use, blocks):
    live_slots = jnp.arange(indices.shape[0]) < in_use
    hits = (indices[:, None] == jnp.arange(blocks)[None, :]) & live_slots[:, None]
    return hits.astype(jnp.float32)


def primal_product(tile_set, places, in_use, extrapolated, row_blocks):
    scenarios = extrapolated.shape[0]
    tile_width = tile_set.shape[-1]
    blocks = extrapolated.reshape(scenarios, -1, tile_width)
    picked = jnp.take(blocks, places[:, 1], axis=1)
    products = jnp.einsum("tij,ktj->kti", tile_set, picked, preferred_element_type=jnp.float32)
    target = pick_matrix(places[:, 0], in_use, row_blocks)
    summed = jnp.einsum("tr,kti->kri", target, products, precision=lax.Precision.HIGHEST)
    return summed.reshape(scenarios, row_blocks * tile_width)


def dual_product(tile_set, places, in_use, dual_half, col_blocks):
    scenarios = dual_half.shape[0]
    tile_width = tile_set.shape[-1]
    blocks = dual_half.reshape(scenarios, -1, tile_width)
    picked = jnp.take(blocks, places[:, 0], axis=1)
    products = jnp.einsum("tij,kti->ktj", tile_set, picked, preferred_element_type=jnp.float32)
    target = pick_matrix(places[:, 1], in_use, col_blocks)
    summed = jnp.einsum("tc,ktj->kcj", target, products, precision=lax.Precision.HIGHEST)
    return summed.reshape(scenarios, col_blocks * tile_width)


def plain(
    tile_values,
    tile_spots,
    tile_counts,
    objective,
    lower_bound,
    bound_span,
    var_kind,
    right_side,
    row_kind,
    primal_start,
    dual_start,
):
    tile_set = tile_values.reshape(tile_values.shape[2:])
    places = tile_spots.reshape(tile_spots.shape[2:])
    in_use = tile_counts.reshape(())
    tile_width = tile_set.shape[-1]
    row_blocks = right_side.shape[1] // tile_width
    col_blocks = objective.shape[0] // tile_width
    row_groups = lax.axis_size("row")
    col_groups = lax.axis_size("col")
    total_rows = right_side.shape[1] * row_groups
    total_cols = objective.shape[0] * col_groups
    upper_bound = lower_bound + bound_span
    objective_squares = lax.psum(jnp.sum(objective * objective), "col")
    objective_scale = jnp.sqrt(objective_squares / total_cols + EPSILON)
    side_squares = jnp.sum(right_side * right_side, axis=1)
    side_total = lax.psum(side_squares, "row")
    weight = objective_scale / jnp.sqrt(side_total / total_rows + EPSILON)
    primal, dual_vec = (primal_start, dual_start)
    dual_stat = side_squares
    primal_total = None
    for iteration in range(ITERS):
        final = iteration == ITERS - 1
        dual_half = dual_vec.astype(jnp.bfloat16)
        partial_gradient = dual_product(tile_set, places, in_use, dual_half, col_blocks)
        gradient = lax.psum(partial_gradient, "row")
        primal_step = (STEP_SCALE / weight)[:, None]
        primal_next = project_primal(
            primal - primal_step * (objective - gradient), lower_bound, upper_bound, var_kind
        )
        extrapolated = (2.0 * primal_next - primal).astype(jnp.bfloat16)
        partial_image = primal_product(tile_set, places, in_use, extrapolated, row_blocks)
        primal_squares = jnp.sum((primal_next - primal_start) ** 2, axis=1)
        image = lax.psum(partial_image, "col")
        dual_step = (STEP_SCALE * weight)[:, None]
        dual_next = project_dual(dual_vec + dual_step * (right_side - image), row_kind)
        dual_stat = jnp.sum((dual_next - dual_start) ** 2, axis=1)
        if not final:
            primal_total = lax.psum(primal_squares, "col")
            dual_total = lax.psum(dual_stat, "row")
            weight = weight_update(weight, primal_total, dual_total, total_cols, total_rows)
        primal, dual_vec = (primal_next, dual_next)
    return (primal, dual_vec)


def kernel(
    n_row,
    n_col,
    chunks,
    tiles_hbm,
    spots,
    counts,
    objective_hbm,
    lower_hbm,
    span_hbm,
    var_kind_hbm,
    right_side_hbm,
    row_kind_hbm,
    primal_start_hbm,
    dual_start_hbm,
    primal_out,
    dual_out,
    tiles,
    objective,
    lower,
    span,
    var_kind,
    right_side,
    row_kind,
    primal_start,
    dual_start,
    sides,
    load_sem,
    matrix,
    matrix_t,
    primal_all,
    dual_all,
    row_send,
    col_send,
    row_mid,
    row_pass,
    row_recv,
    col_recv,
    cost_all,
    cost_total,
    sent,
    row_rs_in,
    row_ag_in,
    col_rs_in,
    col_ag_in,
    cost_out,
    cost_in,
):
    r = lax.axis_index("row")
    c = lax.axis_index("col")
    odd, upper = lax.rem(r, 2), r // 2
    slots, width = tiles.shape[0], tiles.shape[1]
    n_vars = objective.shape[1]
    n_rows = row_kind.shape[1]
    total_cols = n_vars * n_col
    total_rows = n_rows * n_row
    row_blocks, col_blocks = n_rows // width, n_vars // width
    steps = ITERS * chunks
    part = primal_all.shape[1] * SUB

    def row_peer(d):
        return lax.rem(r + d, n_row)

    def col_peer(d):
        return lax.rem(c + d, n_col)

    def row_copy(src, dst, d, out_sem, in_sem):
        return pltpu.make_async_remote_copy(
            src_ref=src, dst_ref=dst, send_sem=out_sem, recv_sem=in_sem,
            device_id={"row": row_peer(d)}, device_id_type=MESH,
        )

    def col_copy(src, dst, d, out_sem, in_sem):
        return pltpu.make_async_remote_copy(
            src_ref=src, dst_ref=dst, send_sem=out_sem, recv_sem=in_sem,
            device_id={"col": col_peer(d)}, device_id_type=MESH,
        )

    def pair_rs(s):
        k = lax.rem(s, chunks)
        return pltpu.make_async_remote_copy(
            src_ref=row_send.at[s, 1 - odd], dst_ref=row_mid.at[s],
            send_sem=sent.at[0], recv_sem=row_rs_in.at[k, 0],
            device_id={"row": r + 1 - 2 * odd}, device_id_type=MESH,
        )

    def half_rs(s):
        k = lax.rem(s, chunks)
        return row_copy(row_pass.at[s], row_recv.at[s], n_row // 2,
                        sent.at[1], row_rs_in.at[k, 1])

    def col_rs(s, d):
        k = lax.rem(s, chunks)
        return col_copy(col_send.at[s, col_peer(d)], col_recv.at[s, d - 1], d,
                        sent.at[3], col_rs_in.at[k])

    def row_ag(s, d):
        k = lax.rem(s, chunks)
        here = primal_all.at[s + chunks, r]
        return row_copy(here, here, d, sent.at[2], row_ag_in.at[k])

    def col_ag(s, d):
        k = lax.rem(s, chunks)
        here = dual_all.at[s + chunks, c]
        return col_copy(here, here, d, sent.at[4], col_ag_in.at[k])

    def bytes_of(ref, sem):
        pltpu.make_async_copy(ref, ref, sem).wait()

    def arrived(sem):
        bytes_of(col_recv.at[0], sem)

    def cost_copy(d):
        return col_copy(cost_all.at[0], cost_all.at[d], d, cost_out.at[d - 1], cost_in.at[d - 1])

    loads = [
        (tiles_hbm, tiles),
        (dual_start_hbm, dual_start),
        (right_side_hbm, right_side),
        (objective_hbm, objective),
        (primal_start_hbm, primal_start),
        (lower_hbm, lower),
        (span_hbm, span),
        (var_kind_hbm, var_kind),
        (row_kind_hbm, row_kind),
    ]
    loads = [pltpu.make_async_copy(src, dst, load_sem.at[i]) for i, (src, dst) in enumerate(loads)]
    for load in loads:
        load.start()

    barrier = pltpu.get_barrier_semaphore()
    for d in range(1, n_row):
        pl.semaphore_signal(barrier, inc=1, device_id={"row": row_peer(d)}, device_id_type=MESH)
    for d in range(1, n_col):
        pl.semaphore_signal(barrier, inc=1, device_id={"col": col_peer(d)}, device_id_type=MESH)

    for k in range(chunks):
        primal_all[k, :, :, n_vars:] = jnp.ones((part // SUB, SUB, LANE), jnp.float32)
        dual_all[k, :, :, n_rows:] = jnp.ones((part // SUB, SUB, LANE), jnp.float32)

    keys = []
    for t in range(slots):
        key = spots[t, 0] * col_blocks + spots[t, 1]
        keys.append(jnp.where(t < counts[0, 0], key, -1))
    loads[0].wait()
    for p in range(row_blocks * col_blocks):
        slot = jnp.int32(0)
        live = jnp.float32(0.0)
        for t in range(slots):
            hit = keys[t] == p
            slot = jnp.where(hit, jnp.int32(t), slot)
            live = jnp.where(hit, jnp.float32(1.0), live)
        rb, cb = p // col_blocks, p % col_blocks
        tile = (tiles[slot].astype(jnp.float32) * live).astype(jnp.bfloat16)
        matrix[rb * width:(rb + 1) * width, cb * width:(cb + 1) * width] = tile

    for load in loads[1:]:
        load.wait()
    costs = objective[...]
    cost_all[0] = jnp.broadcast_to(jnp.sum(costs * costs, axis=1, keepdims=True), (SUB, LANE))

    for k in range(chunks):
        for q in range(n_row):
            rows = slice(k * part + q * SUB, k * part + (q + 1) * SUB)
            primal_all[k, q, :, :n_vars] = primal_start[rows, :]
            dual_all[k, q, :, :n_rows] = dual_start[rows, :]
            sides[k, q] = right_side[rows, :]
    pl.semaphore_wait(barrier, n_row + n_col - 2)
    for d in range(1, n_col):
        cost_copy(d).start()

    def wide(value, width_):
        return jnp.concatenate([value] * (width_ // LANE), axis=1)

    def stacked(value):
        return jnp.concatenate([value[q] for q in range(value.shape[0])], axis=0)

    def gradient_part(s):
        k = lax.rem(s, chunks)
        held = dual_all[s, :, :, :n_rows]
        gap = jnp.where(s < chunks, sides[k], held - dual_all[k, :, :, :n_rows])
        spread = jnp.broadcast_to(jnp.sum(gap * gap, axis=2, keepdims=True), (n_row, SUB, LANE))
        terms = jnp.dot(stacked(held).astype(jnp.bfloat16), matrix[...], preferred_element_type=jnp.float32)
        for q in range(n_row):
            row_send[s, q % 2, q // 2, :, :n_vars] = terms[q * SUB:(q + 1) * SUB]
            row_send[s, q % 2, q // 2, :, n_vars:] = spread[q]
        pair_rs(s).start()

    def pass_on(s):
        pair_rs(s).wait_recv()
        row_pass[s] = row_send[s, odd, 1 - upper] + row_mid[s, 1 - upper]
        half_rs(s).start()

    def primal_step(s):
        half_rs(s).wait_recv()
        total = row_send[s, odd, upper] + row_mid[s, upper] + row_recv[s]
        gradient, dual_total = total[:, :n_vars], total[:, n_vars:]
        held = primal_all[s, r]
        old, old_weight = held[:, :n_vars], held[:, n_vars:]
        primal_total = dual_all[s, r, :, n_rows:]
        dual_spread = jnp.sqrt(dual_total / total_rows + EPSILON)
        scale = jnp.sqrt(cost_total[...] / total_cols + EPSILON)
        primal_spread = jnp.sqrt(primal_total / total_cols + EPSILON)
        later = jnp.sqrt(old_weight * dual_spread / primal_spread)
        weight = jnp.where(s < chunks, scale / dual_spread, later)
        step = wide(STEP_SCALE / weight, n_vars)
        low = lower[...]
        new = old - step * (objective[...] - gradient)
        new = project_primal(new, low, low + span[...], var_kind[...])
        primal_all[s + chunks, r, :, :n_vars] = new
        primal_all[s + chunks, r, :, n_vars:] = weight
        for d in range(1, n_row):
            row_ag(s, d).start()

    def image_part(s):
        k = lax.rem(s, chunks)
        arrived(row_ag_in.at[k])
        new = primal_all[s + chunks, :, :, :n_vars]
        old = primal_all[s, :, :, :n_vars]
        gap = new - primal_all[k, :, :, :n_vars]
        spread = jnp.broadcast_to(jnp.sum(gap * gap, axis=2, keepdims=True), (n_row, SUB, LANE))
        ahead = stacked(2.0 * new - old).astype(jnp.bfloat16)
        terms = jnp.dot(ahead, matrix_t[...], preferred_element_type=jnp.float32)
        for q in range(n_col):
            col_send[s, q, :, :n_rows] = terms[q * SUB:(q + 1) * SUB]
            col_send[s, q, :, n_rows:] = spread[q]
        for d in range(1, n_col):
            col_rs(s, d).start()

        @pl.when(s >= steps - chunks)
        def _():
            primal_out[pl.ds(pl.multiple_of(k * part, part), part), :] = stacked(new)

    def dual_step(s):
        k = lax.rem(s, chunks)
        arrived(col_rs_in.at[k])
        total = col_send[s, c]
        for d in range(1, n_col):
            total = total + col_recv[s, d - 1]
        side = sides[k, c]
        step = wide(STEP_SCALE * primal_all[s + chunks, c, :, n_vars:], n_rows)
        new = dual_all[s, c, :, :n_rows] + step * (side - total[:, :n_rows])
        new = project_dual(new, row_kind[...])
        dual_all[s + chunks, c, :, :n_rows] = new
        dual_all[s + chunks, c, :, n_rows:] = total[:, n_rows:]
        for d in range(1, n_col):
            col_ag(s, d).start()

    def dual_arrive(s):
        arrived(col_ag_in.at[lax.rem(s, chunks)])

        @pl.when(s >= steps - chunks)
        def _():
            k = lax.rem(s, chunks)
            new = stacked(dual_all[s + chunks, :, :, :n_rows])
            dual_out[pl.ds(pl.multiple_of(k * part, part), part), :] = new

    def one_step(t, carry):
        def stage(delay, run):
            @pl.when((t >= delay) & (t < steps + delay))
            def _():
                run(t - delay)

        stage(chunks, dual_arrive)
        stage(0, gradient_part)

        @pl.when(t == 0)
        def _():
            for rb in range(row_blocks):
                for cb in range(col_blocks):
                    tile = matrix[rb * width:(rb + 1) * width, cb * width:(cb + 1) * width]
                    matrix_t[cb * width:(cb + 1) * width, rb * width:(rb + 1) * width] = tile.T
            for d in range(1, n_col):
                cost_copy(d).wait()
            total = cost_all[0]
            for d in range(1, n_col):
                total = total + cost_all[d]
            cost_total[...] = total

        stage(5, image_part)
        stage(3, primal_step)
        stage(1, pass_on)
        stage(6, dual_step)
        return carry

    lax.fori_loop(0, steps + chunks, one_step, 0)
    for i, ref in enumerate([row_mid, row_pass, col_recv, col_recv, col_recv]):
        bytes_of(ref, sent.at[i])


def fused(
    tile_values,
    tile_spots,
    tile_counts,
    objective,
    lower_bound,
    bound_span,
    var_kind,
    right_side,
    row_kind,
    primal_start,
    dual_start,
):
    n_row, n_col = lax.axis_size("row"), lax.axis_size("col")
    scenarios, n_rows = right_side.shape
    n_vars = objective.shape[0]
    owners = n_row
    chunks = scenarios // (SUB * owners)
    steps = ITERS * chunks
    vmem = pl.BlockSpec(memory_space=pltpu.VMEM)
    smem = pl.BlockSpec(memory_space=pltpu.SMEM)
    hbm = pl.BlockSpec(memory_space=pltpu.HBM)
    floats = lambda *shape: pltpu.VMEM(shape, jnp.float32)
    sems = lambda *shape: pltpu.SemaphoreType.DMA(shape)
    wide_v, wide_r = n_vars + LANE, n_rows + LANE
    return pl.pallas_call(
        functools.partial(kernel, n_row, n_col, chunks),
        out_shape=(
            jax.ShapeDtypeStruct(primal_start.shape, jnp.float32),
            jax.ShapeDtypeStruct(dual_start.shape, jnp.float32),
        ),
        in_specs=[hbm, smem, smem] + [hbm] * 8,
        out_specs=(vmem, vmem),
        scratch_shapes=[
            pltpu.VMEM(tile_values.shape[2:], jnp.bfloat16),
            floats(1, n_vars),
            floats(1, n_vars),
            floats(1, n_vars),
            pltpu.VMEM((1, n_vars), jnp.int32),
            floats(*right_side.shape),
            pltpu.VMEM((1, n_rows), jnp.int32),
            floats(*primal_start.shape),
            floats(*dual_start.shape),
            floats(chunks, owners, SUB, n_rows),
            sems(9),
            pltpu.VMEM((n_rows, n_vars), jnp.bfloat16),
            pltpu.VMEM((n_vars, n_rows), jnp.bfloat16),
            floats(steps + chunks, owners, SUB, wide_v),
            floats(steps + chunks, owners, SUB, wide_r),
            floats(steps, 2, n_row // 2, SUB, wide_v),
            floats(steps, owners, SUB, wide_r),
            floats(steps, n_row // 2, SUB, wide_v),
            floats(steps, SUB, wide_v),
            floats(steps, SUB, wide_v),
            floats(steps, n_col - 1, SUB, wide_r),
            floats(n_col, SUB, LANE),
            floats(SUB, LANE),
            sems(5),
            sems(chunks, 2),
            sems(chunks),
            sems(chunks),
            sems(chunks),
            sems(n_col - 1), sems(n_col - 1),
        ],
        compiler_params=pltpu.CompilerParams(
            collective_id=0, has_side_effects=True, vmem_limit_bytes=60 * 2**20
        ),
    )(
        tile_values.reshape(tile_values.shape[2:]),
        tile_spots.reshape(tile_spots.shape[2:]),
        tile_counts,
        objective.reshape(1, -1),
        lower_bound.reshape(1, -1),
        bound_span.reshape(1, -1),
        var_kind.reshape(1, -1),
        right_side,
        row_kind.reshape(1, -1),
        primal_start,
        dual_start,
    )


def local(*args):
    n_row, n_col = lax.axis_size("row"), lax.axis_size("col")
    scenarios = args[7].shape[0]
    square = n_row == n_col and args[3].shape[0] == args[7].shape[1]
    if square and n_row == 4 and scenarios == SUB * n_row * 8:
        return fused(*args)
    return plain(*args)


def solution(mesh):
    placed = (
        P(("lp", "row"), "col", None, None, None),
        P(("lp", "row"), "col", None, None),
        P(("lp", "row"), "col"),
        P(("lp", "col")),
        P(("lp", "col")),
        P(("lp", "col")),
        P(("lp", "col")),
        P("lp", "row"),
        P(("lp", "row")),
        P("lp", "col"),
        P("lp", "row"),
    )
    return jax.shard_map(
        local,
        mesh=mesh,
        in_specs=placed,
        out_specs=(P("lp", "col"), P("lp", "row")),
        check_vma=False,
    )
```

```python
import functools

import jax
import jax.numpy as jnp
from jax import lax
from jax.experimental import pallas as pl
from jax.experimental.pallas import tpu as pltpu
from jax.sharding import PartitionSpec as P

ITERS = 3
STEP_SCALE = 0.4
EPSILON = 1e-06
SUB = 4
LANE = 128
MESH = pl.DeviceIdType.MESH


def project_primal(values, lower_bound, upper_bound, var_kind):
    low_on = (var_kind == 1) | (var_kind == 3)
    high_on = (var_kind == 2) | (var_kind == 3)
    values = jnp.where(low_on, jnp.maximum(values, lower_bound), values)
    return jnp.where(high_on, jnp.minimum(values, upper_bound), values)


def project_dual(values, row_kind):
    return jnp.where(row_kind == 1, jnp.maximum(values, 0.0), values)


def weight_update(weight, primal_squares, dual_squares, total_cols, total_rows):
    primal_spread = jnp.sqrt(primal_squares / total_cols + EPSILON)
    dual_spread = jnp.sqrt(dual_squares / total_rows + EPSILON)
    return jnp.sqrt(weight * dual_spread / primal_spread)


def pick_matrix(indices, in_use, blocks):
    live_slots = jnp.arange(indices.shape[0]) < in_use
    hits = (indices[:, None] == jnp.arange(blocks)[None, :]) & live_slots[:, None]
    return hits.astype(jnp.float32)


def primal_product(tile_set, places, in_use, extrapolated, row_blocks):
    scenarios = extrapolated.shape[0]
    tile_width = tile_set.shape[-1]
    blocks = extrapolated.reshape(scenarios, -1, tile_width)
    picked = jnp.take(blocks, places[:, 1], axis=1)
    products = jnp.einsum("tij,ktj->kti", tile_set, picked, preferred_element_type=jnp.float32)
    target = pick_matrix(places[:, 0], in_use, row_blocks)
    summed = jnp.einsum("tr,kti->kri", target, products, precision=lax.Precision.HIGHEST)
    return summed.reshape(scenarios, row_blocks * tile_width)


def dual_product(tile_set, places, in_use, dual_half, col_blocks):
    scenarios = dual_half.shape[0]
    tile_width = tile_set.shape[-1]
    blocks = dual_half.reshape(scenarios, -1, tile_width)
    picked = jnp.take(blocks, places[:, 0], axis=1)
    products = jnp.einsum("tij,kti->ktj", tile_set, picked, preferred_element_type=jnp.float32)
    target = pick_matrix(places[:, 1], in_use, col_blocks)
    summed = jnp.einsum("tc,ktj->kcj", target, products, precision=lax.Precision.HIGHEST)
    return summed.reshape(scenarios, col_blocks * tile_width)


def plain(
    tile_values,
    tile_spots,
    tile_counts,
    objective,
    lower_bound,
    bound_span,
    var_kind,
    right_side,
    row_kind,
    primal_start,
    dual_start,
):
    tile_set = tile_values.reshape(tile_values.shape[2:])
    places = tile_spots.reshape(tile_spots.shape[2:])
    in_use = tile_counts.reshape(())
    tile_width = tile_set.shape[-1]
    row_blocks = right_side.shape[1] // tile_width
    col_blocks = objective.shape[0] // tile_width
    row_groups = lax.axis_size("row")
    col_groups = lax.axis_size("col")
    total_rows = right_side.shape[1] * row_groups
    total_cols = objective.shape[0] * col_groups
    upper_bound = lower_bound + bound_span
    objective_squares = lax.psum(jnp.sum(objective * objective), "col")
    objective_scale = jnp.sqrt(objective_squares / total_cols + EPSILON)
    side_squares = jnp.sum(right_side * right_side, axis=1)
    side_total = lax.psum(side_squares, "row")
    weight = objective_scale / jnp.sqrt(side_total / total_rows + EPSILON)
    primal, dual_vec = (primal_start, dual_start)
    dual_stat = side_squares
    primal_total = None
    for iteration in range(ITERS):
        final = iteration == ITERS - 1
        dual_half = dual_vec.astype(jnp.bfloat16)
        partial_gradient = dual_product(tile_set, places, in_use, dual_half, col_blocks)
        gradient = lax.psum(partial_gradient, "row")
        primal_step = (STEP_SCALE / weight)[:, None]
        primal_next = project_primal(
            primal - primal_step * (objective - gradient), lower_bound, upper_bound, var_kind
        )
        extrapolated = (2.0 * primal_next - primal).astype(jnp.bfloat16)
        partial_image = primal_product(tile_set, places, in_use, extrapolated, row_blocks)
        primal_squares = jnp.sum((primal_next - primal_start) ** 2, axis=1)
        image = lax.psum(partial_image, "col")
        dual_step = (STEP_SCALE * weight)[:, None]
        dual_next = project_dual(dual_vec + dual_step * (right_side - image), row_kind)
        dual_stat = jnp.sum((dual_next - dual_start) ** 2, axis=1)
        if not final:
            primal_total = lax.psum(primal_squares, "col")
            dual_total = lax.psum(dual_stat, "row")
            weight = weight_update(weight, primal_total, dual_total, total_cols, total_rows)
        primal, dual_vec = (primal_next, dual_next)
    return (primal, dual_vec)


def kernel(
    n_row,
    n_col,
    chunks,
    tiles_hbm,
    spots,
    counts,
    objective_hbm,
    lower_hbm,
    span_hbm,
    var_kind_hbm,
    right_side_hbm,
    row_kind_hbm,
    primal_start_hbm,
    dual_start_hbm,
    primal_out,
    dual_out,
    tiles,
    objective,
    lower,
    span,
    var_kind,
    right_side,
    row_kind,
    primal_start,
    dual_start,
    sides,
    load_sem,
    matrix,
    matrix_t,
    primal_all,
    dual_all,
    row_send,
    col_send,
    row_mid,
    row_pass,
    row_recv,
    col_recv,
    cost_all,
    cost_total,
    sent,
    weight_in,
    row_rs_in,
    row_ag_in,
    col_rs_in,
    col_ag_in,
    cost_out,
    cost_in,
):
    r = lax.axis_index("row")
    c = lax.axis_index("col")
    odd, upper = lax.rem(r, 2), r // 2
    slots, width = tiles.shape[0], tiles.shape[1]
    n_vars = objective.shape[1]
    n_rows = row_kind.shape[1]
    total_cols = n_vars * n_col
    total_rows = n_rows * n_row
    row_blocks, col_blocks = n_rows // width, n_vars // width
    steps = ITERS * chunks
    part = primal_all.shape[1] * SUB

    def row_peer(d):
        return lax.rem(r + d, n_row)

    def col_peer(d):
        return lax.rem(c + d, n_col)

    def row_copy(src, dst, d, out_sem, in_sem):
        return pltpu.make_async_remote_copy(
            src_ref=src, dst_ref=dst, send_sem=out_sem, recv_sem=in_sem,
            device_id={"row": row_peer(d)}, device_id_type=MESH,
        )

    def col_copy(src, dst, d, out_sem, in_sem):
        return pltpu.make_async_remote_copy(
            src_ref=src, dst_ref=dst, send_sem=out_sem, recv_sem=in_sem,
            device_id={"col": col_peer(d)}, device_id_type=MESH,
        )

    def pair_rs(s):
        k = lax.rem(s, chunks)
        return pltpu.make_async_remote_copy(
            src_ref=row_send.at[s, 1 - odd], dst_ref=row_mid.at[s],
            send_sem=sent.at[0], recv_sem=row_rs_in.at[k, 0],
            device_id={"row": r + 1 - 2 * odd}, device_id_type=MESH,
        )

    def half_rs(s):
        k = lax.rem(s, chunks)
        return row_copy(row_pass.at[s], row_recv.at[s], n_row // 2,
                        sent.at[1], row_rs_in.at[k, 1])

    def col_rs(s, d):
        k = lax.rem(s, chunks)
        return col_copy(col_send.at[s, col_peer(d)], col_recv.at[s, d - 1], d,
                        sent.at[3], col_rs_in.at[k])

    def row_ag(s, d):
        k = lax.rem(s, chunks)
        here = primal_all.at[s + chunks, r, :, pl.ds(0, n_vars)]
        return row_copy(here, here, d, sent.at[2], row_ag_in.at[k])

    def weight_copy(s, d):
        here = primal_all.at[s + chunks, r, :, pl.ds(n_vars, LANE)]
        return row_copy(here, here, d, sent.at[5], weight_in.at[lax.rem(s, chunks)])

    def col_ag(s, d):
        k = lax.rem(s, chunks)
        here = dual_all.at[s + chunks, c]
        return col_copy(here, here, d, sent.at[4], col_ag_in.at[k])

    def bytes_of(ref, sem):
        pltpu.make_async_copy(ref, ref, sem).wait()

    def arrived(sem):
        bytes_of(col_recv.at[0], sem)

    def cost_copy(d):
        return col_copy(cost_all.at[0], cost_all.at[d], d, cost_out.at[d - 1], cost_in.at[d - 1])

    loads = [
        (tiles_hbm, tiles),
        (dual_start_hbm, dual_start),
        (right_side_hbm, right_side),
        (objective_hbm, objective),
        (primal_start_hbm, primal_start),
        (lower_hbm, lower),
        (span_hbm, span),
        (var_kind_hbm, var_kind),
        (row_kind_hbm, row_kind),
    ]
    loads = [pltpu.make_async_copy(src, dst, load_sem.at[i]) for i, (src, dst) in enumerate(loads)]
    for load in loads:
        load.start()

    barrier = pltpu.get_barrier_semaphore()
    for d in range(1, n_row):
        pl.semaphore_signal(barrier, inc=1, device_id={"row": row_peer(d)}, device_id_type=MESH)
    for d in range(1, n_col):
        pl.semaphore_signal(barrier, inc=1, device_id={"col": col_peer(d)}, device_id_type=MESH)

    keys = []
    for t in range(slots):
        key = spots[t, 0] * col_blocks + spots[t, 1]
        keys.append(jnp.where(t < counts[0, 0], key, -1))
    loads[0].wait()
    for p in range(row_blocks * col_blocks):
        found = jnp.int32(0)
        for t in range(slots):
            found = jnp.where(keys[t] == p, jnp.int32(t + 1), found)
        live = jnp.where(found > 0, jnp.float32(1.0), jnp.float32(0.0))
        slot = jnp.maximum(found - 1, 0)
        rb, cb = p // col_blocks, p % col_blocks
        tile = (tiles[slot].astype(jnp.float32) * live).astype(jnp.bfloat16)
        matrix[rb * width:(rb + 1) * width, cb * width:(cb + 1) * width] = tile

    for load in loads[1:]:
        load.wait()
    costs = objective[...]
    cost_all[0] = jnp.broadcast_to(jnp.sum(costs * costs, axis=1, keepdims=True), (SUB, LANE))

    pl.semaphore_wait(barrier, n_row + n_col - 2)
    for d in range(1, n_col):
        cost_copy(d).start()

    def wide(value, width_):
        return jnp.concatenate([value] * (width_ // LANE), axis=1)

    def stacked(value):
        return jnp.concatenate([value[q] for q in range(value.shape[0])], axis=0)

    def gradient_part(s):
        k = lax.rem(s, chunks)
        held = dual_all[s, :, :, :n_rows]
        gap = jnp.where(s < chunks, sides[k], held - dual_all[k, :, :, :n_rows])
        spread = jnp.broadcast_to(jnp.sum(gap * gap, axis=2, keepdims=True), (n_row, SUB, LANE))
        terms = jnp.dot(stacked(held).astype(jnp.bfloat16), matrix[...], preferred_element_type=jnp.float32)
        for q in range(n_row):
            row_send[s, q % 2, q // 2, :, :n_vars] = terms[q * SUB:(q + 1) * SUB]
            row_send[s, q % 2, q // 2, :, n_vars:] = spread[q]
        pair_rs(s).start()

    def pass_on(s):
        pair_rs(s).wait_recv()
        row_pass[s] = row_send[s, odd, 1 - upper] + row_mid[s, 1 - upper]
        half_rs(s).start()

    def primal_step(s):
        half_rs(s).wait_recv()
        total = row_send[s, odd, upper] + row_mid[s, upper] + row_recv[s]
        gradient, dual_total = total[:, :n_vars], total[:, n_vars:]
        held = primal_all[s, r]
        old, old_weight = held[:, :n_vars], held[:, n_vars:]
        primal_total = dual_all[s, r, :, n_rows:]
        dual_spread = jnp.sqrt(dual_total / total_rows + EPSILON)
        scale = jnp.sqrt(cost_total[...] / total_cols + EPSILON)
        primal_spread = jnp.sqrt(primal_total / total_cols + EPSILON)
        later = jnp.sqrt(old_weight * dual_spread / primal_spread)
        weight = jnp.where(s < chunks, scale / dual_spread, later)
        step = wide(STEP_SCALE / weight, n_vars)
        low = lower[...]
        new = old - step * (objective[...] - gradient)
        new = project_primal(new, low, low + span[...], var_kind[...])
        primal_all[s + chunks, r, :, :n_vars] = new
        primal_all[s + chunks, r, :, n_vars:] = weight
        for d in range(1, n_row):
            row_ag(s, d).start()

        @pl.when(r == c)
        def _():
            for d in range(1, n_row):
                weight_copy(s, d).start()

    def image_part(s):
        k = lax.rem(s, chunks)
        bytes_of(col_recv.at[0, :, :, pl.ds(0, n_vars)], row_ag_in.at[k])
        new = primal_all[s + chunks, :, :, :n_vars]
        old = primal_all[s, :, :, :n_vars]
        gap = new - primal_all[k, :, :, :n_vars]
        spread = jnp.broadcast_to(jnp.sum(gap * gap, axis=2, keepdims=True), (n_row, SUB, LANE))
        ahead = stacked(2.0 * new - old).astype(jnp.bfloat16)
        terms = jnp.dot(ahead, matrix_t[...], preferred_element_type=jnp.float32)
        for q in range(n_col):
            col_send[s, q, :, :n_rows] = terms[q * SUB:(q + 1) * SUB]
            col_send[s, q, :, n_rows:] = spread[q]
        for d in range(1, n_col):
            col_rs(s, d).start()

        @pl.when(s >= steps - chunks)
        def _():
            primal_out[pl.ds(pl.multiple_of(k * part, part), part), :] = stacked(new)

    def dual_step(s):
        k = lax.rem(s, chunks)
        arrived(col_rs_in.at[k])

        @pl.when(r != c)
        def _():
            bytes_of(primal_all.at[s + chunks, c, :, pl.ds(n_vars, LANE)], weight_in.at[k])

        total = col_send[s, c]
        for d in range(1, n_col):
            total = total + col_recv[s, d - 1]
        side = sides[k, c]
        step = wide(STEP_SCALE * primal_all[s + chunks, c, :, n_vars:], n_rows)
        new = dual_all[s, c, :, :n_rows] + step * (side - total[:, :n_rows])
        new = project_dual(new, row_kind[...])
        dual_all[s + chunks, c, :, :n_rows] = new
        dual_all[s + chunks, c, :, n_rows:] = total[:, n_rows:]
        for d in range(1, n_col):
            col_ag(s, d).start()

    def dual_arrive(s):
        arrived(col_ag_in.at[lax.rem(s, chunks)])

        @pl.when(s >= steps - chunks)
        def _():
            k = lax.rem(s, chunks)
            new = stacked(dual_all[s + chunks, :, :, :n_rows])
            dual_out[pl.ds(pl.multiple_of(k * part, part), part), :] = new

    def one_step(t, carry):
        def stage(delay, run):
            @pl.when((t >= delay) & (t < steps + delay))
            def _():
                run(t - delay)

        @pl.when(t < chunks)
        def _():
            rows = pl.ds(pl.multiple_of(t * part, part), part)
            primal, dual, side = primal_start[rows, :], dual_start[rows, :], right_side[rows, :]
            for q in range(n_row):
                own = slice(q * SUB, (q + 1) * SUB)
                primal_all[t, q, :, :n_vars] = primal[own]
                dual_all[t, q, :, :n_rows] = dual[own]
                sides[t, q] = side[own]
            primal_all[t, :, :, n_vars:] = jnp.ones((n_row, SUB, LANE), jnp.float32)
            dual_all[t, :, :, n_rows:] = jnp.ones((n_col, SUB, LANE), jnp.float32)

        stage(chunks, dual_arrive)
        stage(0, gradient_part)

        @pl.when(t == 1)
        def _():
            for rb in range(row_blocks):
                for cb in range(col_blocks):
                    tile = matrix[rb * width:(rb + 1) * width, cb * width:(cb + 1) * width]
                    matrix_t[cb * width:(cb + 1) * width, rb * width:(rb + 1) * width] = tile.T
            for d in range(1, n_col):
                cost_copy(d).wait()
            total = cost_all[0]
            for d in range(1, n_col):
                total = total + cost_all[d]
            cost_total[...] = total

        stage(5, image_part)
        stage(3, primal_step)
        stage(1, pass_on)
        stage(6, dual_step)
        return carry

    lax.fori_loop(0, steps + chunks, one_step, 0)
    for i, ref in enumerate([row_mid, row_pass, col_recv.at[:, :, :, pl.ds(0, n_vars)], col_recv, col_recv]):
        bytes_of(ref, sent.at[i])

    @pl.when(r == c)
    def _():
        bytes_of(col_recv.at[:, :, :, pl.ds(0, LANE)], sent.at[5])


def fused(
    tile_values,
    tile_spots,
    tile_counts,
    objective,
    lower_bound,
    bound_span,
    var_kind,
    right_side,
    row_kind,
    primal_start,
    dual_start,
):
    n_row, n_col = lax.axis_size("row"), lax.axis_size("col")
    scenarios, n_rows = right_side.shape
    n_vars = objective.shape[0]
    owners = n_row
    chunks = scenarios // (SUB * owners)
    steps = ITERS * chunks
    vmem = pl.BlockSpec(memory_space=pltpu.VMEM)
    smem = pl.BlockSpec(memory_space=pltpu.SMEM)
    hbm = pl.BlockSpec(memory_space=pltpu.HBM)
    floats = lambda *shape: pltpu.VMEM(shape, jnp.float32)
    sems = lambda *shape: pltpu.SemaphoreType.DMA(shape)
    wide_v, wide_r = n_vars + LANE, n_rows + LANE
    return pl.pallas_call(
        functools.partial(kernel, n_row, n_col, chunks),
        out_shape=(
            jax.ShapeDtypeStruct(primal_start.shape, jnp.float32),
            jax.ShapeDtypeStruct(dual_start.shape, jnp.float32),
        ),
        in_specs=[hbm, smem, smem] + [hbm] * 8,
        out_specs=(vmem, vmem),
        scratch_shapes=[
            pltpu.VMEM(tile_values.shape[2:], jnp.bfloat16),
            floats(1, n_vars),
            floats(1, n_vars),
            floats(1, n_vars),
            pltpu.VMEM((1, n_vars), jnp.int32),
            floats(*right_side.shape),
            pltpu.VMEM((1, n_rows), jnp.int32),
            floats(*primal_start.shape),
            floats(*dual_start.shape),
            floats(chunks, owners, SUB, n_rows),
            sems(9),
            pltpu.VMEM((n_rows, n_vars), jnp.bfloat16),
            pltpu.VMEM((n_vars, n_rows), jnp.bfloat16),
            floats(steps + chunks, owners, SUB, wide_v),
            floats(steps + chunks, owners, SUB, wide_r),
            floats(steps, 2, n_row // 2, SUB, wide_v),
            floats(steps, owners, SUB, wide_r),
            floats(steps, n_row // 2, SUB, wide_v),
            floats(steps, SUB, wide_v),
            floats(steps, SUB, wide_v),
            floats(steps, n_col - 1, SUB, wide_r),
            floats(n_col, SUB, LANE),
            floats(SUB, LANE),
            sems(6),
            sems(chunks),
            sems(chunks, 2),
            sems(chunks),
            sems(chunks),
            sems(chunks),
            sems(n_col - 1), sems(n_col - 1),
        ],
        compiler_params=pltpu.CompilerParams(
            collective_id=0, has_side_effects=True, vmem_limit_bytes=60 * 2**20
        ),
    )(
        tile_values.reshape(tile_values.shape[2:]),
        tile_spots.reshape(tile_spots.shape[2:]),
        tile_counts,
        objective.reshape(1, -1),
        lower_bound.reshape(1, -1),
        bound_span.reshape(1, -1),
        var_kind.reshape(1, -1),
        right_side,
        row_kind.reshape(1, -1),
        primal_start,
        dual_start,
    )


def local(*args):
    n_row, n_col = lax.axis_size("row"), lax.axis_size("col")
    scenarios = args[7].shape[0]
    square = n_row == n_col and args[3].shape[0] == args[7].shape[1]
    if square and n_row == 4 and scenarios == SUB * n_row * 8:
        return fused(*args)
    return plain(*args)


def solution(mesh):
    placed = (
        P(("lp", "row"), "col", None, None, None),
        P(("lp", "row"), "col", None, None),
        P(("lp", "row"), "col"),
        P(("lp", "col")),
        P(("lp", "col")),
        P(("lp", "col")),
        P(("lp", "col")),
        P("lp", "row"),
        P(("lp", "row")),
        P("lp", "col"),
        P("lp", "row"),
    )
    return jax.shard_map(
        local,
        mesh=mesh,
        in_specs=placed,
        out_specs=(P("lp", "col"), P("lp", "row")),
        check_vma=False,
    )
```

```python
import functools

import jax
import jax.numpy as jnp
from jax import lax
from jax.experimental import pallas as pl
from jax.experimental.pallas import tpu as pltpu
from jax.sharding import PartitionSpec as P

ITERS = 3
STEP_SCALE = 0.4
EPSILON = 1e-06
SUB = 4
LANE = 128
MESH = pl.DeviceIdType.MESH


def project_primal(values, lower_bound, upper_bound, var_kind):
    low_on = (var_kind == 1) | (var_kind == 3)
    high_on = (var_kind == 2) | (var_kind == 3)
    values = jnp.where(low_on, jnp.maximum(values, lower_bound), values)
    return jnp.where(high_on, jnp.minimum(values, upper_bound), values)


def project_dual(values, row_kind):
    return jnp.where(row_kind == 1, jnp.maximum(values, 0.0), values)


def weight_update(weight, primal_squares, dual_squares, total_cols, total_rows):
    primal_spread = jnp.sqrt(primal_squares / total_cols + EPSILON)
    dual_spread = jnp.sqrt(dual_squares / total_rows + EPSILON)
    return jnp.sqrt(weight * dual_spread / primal_spread)


def pick_matrix(indices, in_use, blocks):
    live_slots = jnp.arange(indices.shape[0]) < in_use
    hits = (indices[:, None] == jnp.arange(blocks)[None, :]) & live_slots[:, None]
    return hits.astype(jnp.float32)


def primal_product(tile_set, places, in_use, extrapolated, row_blocks):
    scenarios = extrapolated.shape[0]
    tile_width = tile_set.shape[-1]
    blocks = extrapolated.reshape(scenarios, -1, tile_width)
    picked = jnp.take(blocks, places[:, 1], axis=1)
    products = jnp.einsum("tij,ktj->kti", tile_set, picked, preferred_element_type=jnp.float32)
    target = pick_matrix(places[:, 0], in_use, row_blocks)
    summed = jnp.einsum("tr,kti->kri", target, products, precision=lax.Precision.HIGHEST)
    return summed.reshape(scenarios, row_blocks * tile_width)


def dual_product(tile_set, places, in_use, dual_half, col_blocks):
    scenarios = dual_half.shape[0]
    tile_width = tile_set.shape[-1]
    blocks = dual_half.reshape(scenarios, -1, tile_width)
    picked = jnp.take(blocks, places[:, 0], axis=1)
    products = jnp.einsum("tij,kti->ktj", tile_set, picked, preferred_element_type=jnp.float32)
    target = pick_matrix(places[:, 1], in_use, col_blocks)
    summed = jnp.einsum("tc,ktj->kcj", target, products, precision=lax.Precision.HIGHEST)
    return summed.reshape(scenarios, col_blocks * tile_width)


def plain(
    tile_values,
    tile_spots,
    tile_counts,
    objective,
    lower_bound,
    bound_span,
    var_kind,
    right_side,
    row_kind,
    primal_start,
    dual_start,
):
    tile_set = tile_values.reshape(tile_values.shape[2:])
    places = tile_spots.reshape(tile_spots.shape[2:])
    in_use = tile_counts.reshape(())
    tile_width = tile_set.shape[-1]
    row_blocks = right_side.shape[1] // tile_width
    col_blocks = objective.shape[0] // tile_width
    row_groups = lax.axis_size("row")
    col_groups = lax.axis_size("col")
    total_rows = right_side.shape[1] * row_groups
    total_cols = objective.shape[0] * col_groups
    upper_bound = lower_bound + bound_span
    objective_squares = lax.psum(jnp.sum(objective * objective), "col")
    objective_scale = jnp.sqrt(objective_squares / total_cols + EPSILON)
    side_squares = jnp.sum(right_side * right_side, axis=1)
    side_total = lax.psum(side_squares, "row")
    weight = objective_scale / jnp.sqrt(side_total / total_rows + EPSILON)
    primal, dual_vec = (primal_start, dual_start)
    dual_stat = side_squares
    primal_total = None
    for iteration in range(ITERS):
        final = iteration == ITERS - 1
        dual_half = dual_vec.astype(jnp.bfloat16)
        partial_gradient = dual_product(tile_set, places, in_use, dual_half, col_blocks)
        gradient = lax.psum(partial_gradient, "row")
        primal_step = (STEP_SCALE / weight)[:, None]
        primal_next = project_primal(
            primal - primal_step * (objective - gradient), lower_bound, upper_bound, var_kind
        )
        extrapolated = (2.0 * primal_next - primal).astype(jnp.bfloat16)
        partial_image = primal_product(tile_set, places, in_use, extrapolated, row_blocks)
        primal_squares = jnp.sum((primal_next - primal_start) ** 2, axis=1)
        image = lax.psum(partial_image, "col")
        dual_step = (STEP_SCALE * weight)[:, None]
        dual_next = project_dual(dual_vec + dual_step * (right_side - image), row_kind)
        dual_stat = jnp.sum((dual_next - dual_start) ** 2, axis=1)
        if not final:
            primal_total = lax.psum(primal_squares, "col")
            dual_total = lax.psum(dual_stat, "row")
            weight = weight_update(weight, primal_total, dual_total, total_cols, total_rows)
        primal, dual_vec = (primal_next, dual_next)
    return (primal, dual_vec)


def kernel(
    n_row,
    n_col,
    chunks,
    tiles_hbm,
    spots,
    counts,
    objective_hbm,
    lower_hbm,
    span_hbm,
    var_kind_hbm,
    right_side_hbm,
    row_kind_hbm,
    primal_start_hbm,
    dual_start_hbm,
    primal_out,
    dual_out,
    tiles,
    objective,
    lower,
    span,
    var_kind,
    right_side,
    row_kind,
    primal_start,
    dual_start,
    sides,
    load_sem,
    matrix,
    matrix_t,
    primal_all,
    dual_all,
    row_send,
    col_send,
    row_mid,
    row_pass,
    row_recv,
    col_recv,
    cost_all,
    cost_total,
    sent,
    weight_in,
    row_rs_in,
    row_ag_in,
    col_rs_in,
    col_ag_in,
    cost_out,
    cost_in,
):
    r = lax.axis_index("row")
    c = lax.axis_index("col")
    odd, upper = lax.rem(r, 2), r // 2
    slots, width = tiles.shape[0], tiles.shape[1]
    n_vars = objective.shape[1]
    n_rows = row_kind.shape[1]
    total_cols = n_vars * n_col
    total_rows = n_rows * n_row
    row_blocks, col_blocks = n_rows // width, n_vars // width
    steps = ITERS * chunks
    part = primal_all.shape[1] * SUB

    def row_peer(d):
        return lax.rem(r + d, n_row)

    def col_peer(d):
        return lax.rem(c + d, n_col)

    def row_copy(src, dst, d, out_sem, in_sem):
        return pltpu.make_async_remote_copy(
            src_ref=src, dst_ref=dst, send_sem=out_sem, recv_sem=in_sem,
            device_id={"row": row_peer(d)}, device_id_type=MESH,
        )

    def col_copy(src, dst, d, out_sem, in_sem):
        return pltpu.make_async_remote_copy(
            src_ref=src, dst_ref=dst, send_sem=out_sem, recv_sem=in_sem,
            device_id={"col": col_peer(d)}, device_id_type=MESH,
        )

    def pair_rs(s):
        k = lax.rem(s, chunks)
        return pltpu.make_async_remote_copy(
            src_ref=row_send.at[s, 1 - odd], dst_ref=row_mid.at[s],
            send_sem=sent.at[0], recv_sem=row_rs_in.at[k, 0],
            device_id={"row": r + 1 - 2 * odd}, device_id_type=MESH,
        )

    def half_rs(s):
        k = lax.rem(s, chunks)
        return row_copy(row_pass.at[s], row_recv.at[s], n_row // 2,
                        sent.at[1], row_rs_in.at[k, 1])

    def col_rs(s, d):
        k = lax.rem(s, chunks)
        return col_copy(col_send.at[s, col_peer(d)], col_recv.at[s, d - 1], d,
                        sent.at[3], col_rs_in.at[k])

    def row_ag(s, d):
        k = lax.rem(s, chunks)
        here = primal_all.at[s + chunks, r, :, pl.ds(0, n_vars)]
        return row_copy(here, here, d, sent.at[2], row_ag_in.at[k])

    def weight_copy(s, d):
        here = primal_all.at[s + chunks, r, :, pl.ds(n_vars, LANE)]
        return row_copy(here, here, d, sent.at[5], weight_in.at[lax.rem(s, chunks)])

    def col_ag(s, d):
        k = lax.rem(s, chunks)
        here = dual_all.at[s + chunks, c]
        return col_copy(here, here, d, sent.at[4], col_ag_in.at[k])

    def bytes_of(ref, sem):
        pltpu.make_async_copy(ref, ref, sem).wait()

    def arrived(sem):
        bytes_of(col_recv.at[0], sem)

    def cost_copy(d):
        return col_copy(cost_all.at[0], cost_all.at[d], d, cost_out.at[d - 1], cost_in.at[d - 1])

    loads = [
        (tiles_hbm, tiles),
        (dual_start_hbm, dual_start),
        (right_side_hbm, right_side),
        (objective_hbm, objective),
        (primal_start_hbm, primal_start),
        (lower_hbm, lower),
        (span_hbm, span),
        (var_kind_hbm, var_kind),
        (row_kind_hbm, row_kind),
    ]
    loads = [pltpu.make_async_copy(src, dst, load_sem.at[i]) for i, (src, dst) in enumerate(loads)]
    for load in loads:
        load.start()

    barrier = pltpu.get_barrier_semaphore()
    for d in range(1, n_row):
        pl.semaphore_signal(barrier, inc=1, device_id={"row": row_peer(d)}, device_id_type=MESH)
    for d in range(1, n_col):
        pl.semaphore_signal(barrier, inc=1, device_id={"col": col_peer(d)}, device_id_type=MESH)

    keys = []
    for t in range(slots):
        key = spots[t, 0] * col_blocks + spots[t, 1]
        keys.append(jnp.where(t < counts[0, 0], key, -1))
    loads[0].wait()
    for p in range(row_blocks * col_blocks):
        found = jnp.int32(0)
        for t in range(slots):
            found = jnp.where(keys[t] == p, jnp.int32(t + 1), found)
        live = jnp.where(found > 0, jnp.float32(1.0), jnp.float32(0.0))
        slot = jnp.maximum(found - 1, 0)
        rb, cb = p // col_blocks, p % col_blocks
        tile = (tiles[slot].astype(jnp.float32) * live).astype(jnp.bfloat16)
        matrix[rb * width:(rb + 1) * width, cb * width:(cb + 1) * width] = tile

    for load in loads[1:]:
        load.wait()
    costs = objective[...]
    cost_all[0] = jnp.broadcast_to(jnp.sum(costs * costs, axis=1, keepdims=True), (SUB, LANE))

    pl.semaphore_wait(barrier, n_row + n_col - 2)
    for d in range(1, n_col):
        cost_copy(d).start()

    def wide(value, width_):
        return jnp.concatenate([value] * (width_ // LANE), axis=1)

    def stacked(value):
        return jnp.concatenate([value[q] for q in range(value.shape[0])], axis=0)

    def gradient_part(s):
        k = lax.rem(s, chunks)
        held = dual_all[s, :, :, :n_rows]
        gap = jnp.where(s < chunks, sides[k], held - dual_all[k, :, :, :n_rows])
        spread = jnp.broadcast_to(jnp.sum(gap * gap, axis=2, keepdims=True), (n_row, SUB, LANE))
        terms = jnp.dot(stacked(held).astype(jnp.bfloat16), matrix[...], preferred_element_type=jnp.float32)
        for q in range(n_row):
            row_send[s, q % 2, q // 2, :, :n_vars] = terms[q * SUB:(q + 1) * SUB]
            row_send[s, q % 2, q // 2, :, n_vars:] = spread[q]
        pair_rs(s).start()

    def pass_on(s):
        pair_rs(s).wait_recv()
        row_pass[s] = row_send[s, odd, 1 - upper] + row_mid[s, 1 - upper]
        half_rs(s).start()

    def primal_step(s):
        half_rs(s).wait_recv()
        total = row_send[s, odd, upper] + row_mid[s, upper] + row_recv[s]
        gradient, dual_total = total[:, :n_vars], total[:, n_vars:]
        held = primal_all[s, r]
        old, old_weight = held[:, :n_vars], held[:, n_vars:]
        primal_total = dual_all[s, r, :, n_rows:]
        dual_spread = jnp.sqrt(dual_total / total_rows + EPSILON)
        scale = jnp.sqrt(cost_total[...] / total_cols + EPSILON)
        primal_spread = jnp.sqrt(primal_total / total_cols + EPSILON)
        later = jnp.sqrt(old_weight * dual_spread / primal_spread)
        weight = jnp.where(s < chunks, scale / dual_spread, later)
        step = wide(STEP_SCALE / weight, n_vars)
        low = lower[...]
        new = old - step * (objective[...] - gradient)
        new = project_primal(new, low, low + span[...], var_kind[...])
        primal_all[s + chunks, r, :, :n_vars] = new
        primal_all[s + chunks, r, :, n_vars:] = weight
        for d in range(1, n_row):
            row_ag(s, jnp.where(upper == 0, n_row - d, d)).start()

        @pl.when(r == c)
        def _():
            for d in range(1, n_row):
                weight_copy(s, d).start()

    def image_part(s):
        k = lax.rem(s, chunks)
        bytes_of(col_recv.at[0, :, :, pl.ds(0, n_vars)], row_ag_in.at[k])
        new = primal_all[s + chunks, :, :, :n_vars]
        old = primal_all[s, :, :, :n_vars]
        gap = new - primal_all[k, :, :, :n_vars]
        spread = jnp.broadcast_to(jnp.sum(gap * gap, axis=2, keepdims=True), (n_row, SUB, LANE))
        ahead = stacked(2.0 * new - old).astype(jnp.bfloat16)
        terms = jnp.dot(ahead, matrix_t[...], preferred_element_type=jnp.float32)
        for q in range(n_col):
            col_send[s, q, :, :n_rows] = terms[q * SUB:(q + 1) * SUB]
            col_send[s, q, :, n_rows:] = spread[q]
        for d in range(1, n_col):
            col_rs(s, d).start()

        @pl.when(s >= steps - chunks)
        def _():
            primal_out[pl.ds(pl.multiple_of(k * part, part), part), :] = stacked(new)

    def dual_step(s):
        k = lax.rem(s, chunks)
        arrived(col_rs_in.at[k])

        @pl.when(r != c)
        def _():
            bytes_of(primal_all.at[s + chunks, c, :, pl.ds(n_vars, LANE)], weight_in.at[k])

        total = col_send[s, c]
        for d in range(1, n_col):
            total = total + col_recv[s, d - 1]
        side = sides[k, c]
        step = wide(STEP_SCALE * primal_all[s + chunks, c, :, n_vars:], n_rows)
        new = dual_all[s, c, :, :n_rows] + step * (side - total[:, :n_rows])
        new = project_dual(new, row_kind[...])
        dual_all[s + chunks, c, :, :n_rows] = new
        dual_all[s + chunks, c, :, n_rows:] = total[:, n_rows:]
        for d in range(1, n_col):
            col_ag(s, d).start()

    def dual_arrive(s):
        arrived(col_ag_in.at[lax.rem(s, chunks)])

        @pl.when(s >= steps - chunks)
        def _():
            k = lax.rem(s, chunks)
            new = stacked(dual_all[s + chunks, :, :, :n_rows])
            dual_out[pl.ds(pl.multiple_of(k * part, part), part), :] = new

    def one_step(t, carry):
        def stage(delay, run):
            @pl.when((t >= delay) & (t < steps + delay))
            def _():
                run(t - delay)

        @pl.when(t < chunks)
        def _():
            rows = pl.ds(pl.multiple_of(t * part, part), part)
            primal, dual, side = primal_start[rows, :], dual_start[rows, :], right_side[rows, :]
            for q in range(n_row):
                own = slice(q * SUB, (q + 1) * SUB)
                primal_all[t, q, :, :n_vars] = primal[own]
                dual_all[t, q, :, :n_rows] = dual[own]
                sides[t, q] = side[own]
            primal_all[t, :, :, n_vars:] = jnp.ones((n_row, SUB, LANE), jnp.float32)
            dual_all[t, :, :, n_rows:] = jnp.ones((n_col, SUB, LANE), jnp.float32)

        stage(chunks, dual_arrive)
        stage(0, gradient_part)

        @pl.when(t == 1)
        def _():
            for rb in range(row_blocks):
                for cb in range(col_blocks):
                    tile = matrix[rb * width:(rb + 1) * width, cb * width:(cb + 1) * width]
                    matrix_t[cb * width:(cb + 1) * width, rb * width:(rb + 1) * width] = tile.T
            for d in range(1, n_col):
                cost_copy(d).wait()
            total = cost_all[0]
            for d in range(1, n_col):
                total = total + cost_all[d]
            cost_total[...] = total

        stage(5, image_part)
        stage(3, primal_step)
        stage(1, pass_on)
        stage(6, dual_step)
        return carry

    lax.fori_loop(0, steps + chunks, one_step, 0)
    for i, ref in enumerate([row_mid, row_pass, col_recv.at[:, :, :, pl.ds(0, n_vars)], col_recv, col_recv]):
        bytes_of(ref, sent.at[i])

    @pl.when(r == c)
    def _():
        bytes_of(col_recv.at[:, :, :, pl.ds(0, LANE)], sent.at[5])


def fused(
    tile_values,
    tile_spots,
    tile_counts,
    objective,
    lower_bound,
    bound_span,
    var_kind,
    right_side,
    row_kind,
    primal_start,
    dual_start,
):
    n_row, n_col = lax.axis_size("row"), lax.axis_size("col")
    scenarios, n_rows = right_side.shape
    n_vars = objective.shape[0]
    owners = n_row
    chunks = scenarios // (SUB * owners)
    steps = ITERS * chunks
    vmem = pl.BlockSpec(memory_space=pltpu.VMEM)
    smem = pl.BlockSpec(memory_space=pltpu.SMEM)
    hbm = pl.BlockSpec(memory_space=pltpu.HBM)
    floats = lambda *shape: pltpu.VMEM(shape, jnp.float32)
    sems = lambda *shape: pltpu.SemaphoreType.DMA(shape)
    wide_v, wide_r = n_vars + LANE, n_rows + LANE
    return pl.pallas_call(
        functools.partial(kernel, n_row, n_col, chunks),
        out_shape=(
            jax.ShapeDtypeStruct(primal_start.shape, jnp.float32),
            jax.ShapeDtypeStruct(dual_start.shape, jnp.float32),
        ),
        in_specs=[hbm, smem, smem] + [hbm] * 8,
        out_specs=(vmem, vmem),
        scratch_shapes=[
            pltpu.VMEM(tile_values.shape[2:], jnp.bfloat16),
            floats(1, n_vars),
            floats(1, n_vars),
            floats(1, n_vars),
            pltpu.VMEM((1, n_vars), jnp.int32),
            floats(*right_side.shape),
            pltpu.VMEM((1, n_rows), jnp.int32),
            floats(*primal_start.shape),
            floats(*dual_start.shape),
            floats(chunks, owners, SUB, n_rows),
            sems(9),
            pltpu.VMEM((n_rows, n_vars), jnp.bfloat16),
            pltpu.VMEM((n_vars, n_rows), jnp.bfloat16),
            floats(steps + chunks, owners, SUB, wide_v),
            floats(steps + chunks, owners, SUB, wide_r),
            floats(steps, 2, n_row // 2, SUB, wide_v),
            floats(steps, owners, SUB, wide_r),
            floats(steps, n_row // 2, SUB, wide_v),
            floats(steps, SUB, wide_v),
            floats(steps, SUB, wide_v),
            floats(steps, n_col - 1, SUB, wide_r),
            floats(n_col, SUB, LANE),
            floats(SUB, LANE),
            sems(6),
            sems(chunks),
            sems(chunks, 2),
            sems(chunks),
            sems(chunks),
            sems(chunks),
            sems(n_col - 1), sems(n_col - 1),
        ],
        compiler_params=pltpu.CompilerParams(
            collective_id=0, has_side_effects=True, vmem_limit_bytes=60 * 2**20
        ),
    )(
        tile_values.reshape(tile_values.shape[2:]),
        tile_spots.reshape(tile_spots.shape[2:]),
        tile_counts,
        objective.reshape(1, -1),
        lower_bound.reshape(1, -1),
        bound_span.reshape(1, -1),
        var_kind.reshape(1, -1),
        right_side,
        row_kind.reshape(1, -1),
        primal_start,
        dual_start,
    )


def local(*args):
    n_row, n_col = lax.axis_size("row"), lax.axis_size("col")
    scenarios = args[7].shape[0]
    square = n_row == n_col and args[3].shape[0] == args[7].shape[1]
    if square and n_row == 4 and scenarios == SUB * n_row * 8:
        return fused(*args)
    return plain(*args)


def solution(mesh):
    placed = (
        P(("lp", "row"), "col", None, None, None),
        P(("lp", "row"), "col", None, None),
        P(("lp", "row"), "col"),
        P(("lp", "col")),
        P(("lp", "col")),
        P(("lp", "col")),
        P(("lp", "col")),
        P("lp", "row"),
        P(("lp", "row")),
        P("lp", "col"),
        P("lp", "row"),
    )
    return jax.shard_map(
        local,
        mesh=mesh,
        in_specs=placed,
        out_specs=(P("lp", "col"), P("lp", "row")),
        check_vma=False,
    )
```
